512 devices in a mesh: box: 64 (over y, z_lo, core), ang: 8 (over z_hi, x).
Axes of the slice: x: 4, y: 4, z: 16 (z_hi: 2, z_lo: 8; z = z_hi * 8 + z_lo), core: 2. Of those that a mesh axis runs over, the one named last changes fastest.
Arguments:
- coeffs: bfloat16 [8, 576, 2, 8192], P('ang', None, None, 'box'), may hold values from -6 to 6
- freqs: bfloat16 [8, 5, 2, 8192], P('ang', None, None, 'box'), may hold values from -6 to 6
- nodes: float32 [4, 3, 2, 576], replicated, may hold values from -0.5 to 0.5
- centres: float32 [4, 3, 2, 64], replicated, may hold values from -2 to 2
- interp: bfloat16 [2, 576, 576], replicated, may hold values from -0.1875 to 0.1875
- evaluate: bfloat16 [1024, 576], replicated, may hold values from -0.09375 to 0.09375
Outputs:
- image_slice: float32 [1024, 8192], P('ang', 'box')
The draws below stay inside these ranges and needn't reach their ends.
All inputs are finite; a program needn't handle non-finite values.
Results may differ from the reference program's by a relative error of at most 0.015.
Values may be sent and summed in bfloat16 or wider, within the bound.
No kernel may reach another device: no remote copies, remote signals or barrier semaphores. Data moves between devices by JAX's collectives and lax.ppermute only.
A program may use at most 192 MiB of HBM per device.

```python
import jax
import jax.numpy as jnp
from jax import lax

Q = 24
R2 = 576
SECTIONS = 4
F_DEV = 128
PIX = 1024
BLOCKS = 8
COLS = 8192
N_BOX = 64


def level_of(key, extent, cuts, least, high):
    gain = 1.0
    for axis_at, shards_of in cuts:
        draws = jax.random.uniform(jax.random.fold_in(jax.random.fold_in(key, 6), axis_at), (shards_of,), jnp.float32, least / len(cuts), high / len(cuts))
        gain = gain * jnp.repeat(jnp.exp(draws), extent[axis_at] // shards_of).reshape((-1,) + (1,) * (len(extent) - 1 - axis_at))
    return gain


def normal_values(stream_key, dims, spread, bound, split=(), held_as=jnp.bfloat16):
    entries = jax.random.normal(stream_key, dims, jnp.float32) * spread
    if len(split) > 0:
        entries = level_of(stream_key, dims, split, -0.22, 0.18) * entries
    return jnp.clip(entries, min=-bound, max=bound).astype(held_as)


def setup_inputs(seed: int = 0) -> dict:
    arg_keys = jax.random.split(jax.random.key(seed), 7)
    coeffs = normal_values(arg_keys[0], (BLOCKS, R2, 2, COLS), 1.0, 6.0, ((0, 8), (3, 64)))
    freqs = jnp.clip(jax.random.uniform(arg_keys[1], (BLOCKS, SECTIONS + 1, 2, COLS), jnp.float32, -6.0, 6.0) * level_of(arg_keys[1], (BLOCKS, SECTIONS + 1, 2, COLS), ((0, 8), (3, 64)), -0.4, 0.0), -6.0, 6.0).astype(jnp.bfloat16)
    nodes = jnp.clip(jax.random.uniform(arg_keys[2], (SECTIONS, 3, 2, R2), jnp.float32, -0.5, 0.5), -0.5, 0.5)
    centres = jnp.clip(jax.random.uniform(arg_keys[3], (SECTIONS, 3, 2, N_BOX), jnp.float32, -2.0, 2.0), -2.0, 2.0)
    interp = normal_values(arg_keys[4], (2, R2, R2), (2 * Q * Q) ** -0.5, 0.1875)
    evaluate = normal_values(arg_keys[5], (PIX, R2), (Q * Q * BLOCKS) ** -0.5, 0.09375)
    return {"coeffs": coeffs, "freqs": freqs, "nodes": nodes, "centres": centres, "interp": interp, "evaluate": evaluate}


def angle(rel_two, cen_two, freq_two):
    first = (rel_two[0][:, None] + cen_two[0][None, :]) * freq_two[0][None, :]
    second = (rel_two[1][:, None] + cen_two[1][None, :]) * freq_two[1][None, :]
    return first + second


def rotate(values, phase):
    real_part = values[:, 0].astype(jnp.float32)
    imag_part = values[:, 1].astype(jnp.float32)
    cosine = jnp.cos(phase)
    sine = jnp.sin(phase)
    return jnp.stack([cosine * real_part - sine * imag_part, sine * real_part + cosine * imag_part], axis=1)


def section_core(own, other, bits, rel_s, cen_s, freq_s, interp):
    coeff_count = own.shape[0]
    width = own.shape[2]
    lower_self = (bits == 0)[None, None, :]
    lower = jnp.where(lower_self, own, other)
    upper = jnp.where(lower_self, other, own)
    w_low = rotate(lower, -angle(rel_s[0], cen_s[0], freq_s)).astype(jnp.bfloat16)
    w_high = rotate(upper, -angle(rel_s[1], cen_s[1], freq_s)).astype(jnp.bfloat16)
    total = jnp.dot(interp[0], w_low.reshape(coeff_count, 2 * width), preferred_element_type=jnp.float32)
    total = total + jnp.dot(interp[1], w_high.reshape(coeff_count, 2 * width), preferred_element_type=jnp.float32)
    return rotate(total.reshape(coeff_count, 2, width), angle(rel_s[2], cen_s[2], freq_s)).astype(jnp.bfloat16)


def reference(coeffs, freqs, nodes, centres, interp, evaluate):
    cen_cols = jnp.repeat(centres, F_DEV, axis=3)
    box_of = (jnp.arange(COLS) // F_DEV).astype(jnp.int32)
    offsets = jnp.arange(F_DEV).astype(jnp.int32)

    def one_block(carry, blocks):
        field, freq = blocks
        for level in range(SECTIONS):
            partner_box = (jnp.arange(N_BOX).astype(jnp.int32) ^ (1 << level)).astype(jnp.int32)
            columns = (partner_box[:, None] * F_DEV + offsets[None, :]).reshape(-1)
            other = jnp.take(field, columns, axis=2)
            bits = (box_of >> level) & 1
            field = section_core(field, other, bits, nodes[level], cen_cols[level], freq[level].astype(jnp.float32), interp)
        phase = angle(nodes[SECTIONS - 1, 2], cen_cols[SECTIONS - 1, 2], freq[SECTIONS].astype(jnp.float32))
        values = (jnp.cos(phase) * field[:, 0].astype(jnp.float32) - jnp.sin(phase) * field[:, 1].astype(jnp.float32)).astype(jnp.bfloat16)
        return carry + jnp.dot(evaluate, values, preferred_element_type=jnp.float32), None

    start = jnp.zeros((PIX, COLS), jnp.float32)
    image_slice, unused = lax.scan(one_block, start, (coeffs, freqs))
    return image_slice
```

```python
import jax
import jax.numpy as jnp
import numpy as np
from jax import lax
from jax.experimental import pallas as pl
from jax.experimental.pallas import tpu as pltpu
from jax.sharding import Mesh, PartitionSpec as P

AXES = ("y", "z4", "z2", "z1", "c", "zh", "x")
SIZES = (4, 2, 2, 2, 2, 2, 4)
NEAR = ("z2", "z1", "c", "x")
FAR = ("z4",) + NEAR
ALL = ("z4", "z2", "z1", "c", "zh", "x")
K = 576
COLS = 128
PIX = 1024
F32 = jnp.float32
BF16 = jnp.bfloat16

COS = (
    0.999999989059023,
    -19.739204499453944,
    64.9391174598965,
    -85.45013953089278,
    60.16763095097771,
    -25.96759924841038,
    6.5286581610231424,
)
SIN = (
    6.283184916495431,
    -41.34158923268858,
    81.59994332978287,
    -76.61447253124996,
    41.34288235456833,
    -12.471243535026977,
)


def horner(coefficients, u):
    total = u * coefficients[-1] + coefficients[-2]
    for value in coefficients[-3::-1]:
        total = total * u + value
    return total


def cos_sin(turns):
    r = turns - jnp.floor(turns + 0.5)
    u = r * r
    return horner(COS, u), r * horner(SIN, u)


def trig_kernel(where_ref, freq_ref, nodes_ref, cen_ref, cos_ref, sin_ref, g_ref, c_ref):
    base = where_ref[0] * 16
    half = where_ref[1]
    row = lax.broadcasted_iota(jnp.int32, (COLS, 64), 0) // 16
    lane = lax.broadcasted_iota(jnp.int32, (COLS, 64), 1)
    for t in range(2):
        hot = jnp.where(lane == row + (base + t * 8), 1.0, 0.0).astype(F32)
        c_ref[t] = lax.dot_general(
            hot,
            cen_ref[...],
            (((1,), (1,)), ((), ())),
            precision=lax.Precision.HIGHEST,
            preferred_element_type=F32,
        )
        g_ref[t] = freq_ref[t].astype(F32) * (0.5 / np.pi)

    def node(level, kind, d):
        i = (level * 3 + kind) * 2 + d
        return nodes_ref[i : i + 1, :]

    def cen(block, level, kind, d):
        i = (level * 3 + kind) * 2 + d
        return block[:, i : i + 1]

    def fr(block, level, d):
        i = level * 2 + d
        return block[:, i : i + 1]

    low_side = half == 0

    @pl.loop(0, 16)
    def _(i):
        here = pl.ds(pl.multiple_of(i * 8, 8), 8)

        def store(index, turns):
            c, s = cos_sin(turns)
            cos_ref[index, here, :] = c
            sin_ref[index, here, :] = s

        def phase(level, kind, g, cc):
            fx, fy = fr(g, level, 0), fr(g, level, 1)
            const = cen(cc, level, kind, 0) * fx + cen(cc, level, kind, 1) * fy
            return node(level, kind, 0) * fx + node(level, kind, 1) * fy + const

        g_own, c_own = g_ref[half, here, :], c_ref[half, here, :]
        for kind in range(2):
            store(kind, -phase(0, kind, g_own, c_own))
        for level in range(1, 3):
            bit = 2 << level
            for kind in range(2):
                src = (i & ~bit) | (bit * kind)
                there = pl.ds(pl.multiple_of(src * 8, 8), 8)
                up = phase(level - 1, 2, g_ref[half, there, :], c_ref[half, there, :])
                store(2 * level + kind, up - phase(level, kind, g_own, c_own))
        up = phase(2, 2, g_own, c_own)
        for t in range(2):
            g, cc = g_ref[t, here, :], c_ref[t, here, :]
            down = jnp.where(low_side, phase(3, 0, g, cc), phase(3, 1, g, cc))
            store(6 + t, up - down)
            fx = fr(g, 3, 0) + fr(g, 4, 0)
            fy = fr(g, 3, 1) + fr(g, 4, 1)
            const = cen(cc, 3, 2, 0) * fx + cen(cc, 3, 2, 1) * fy
            store(8 + t, node(3, 2, 0) * fx + node(3, 2, 1) * fy + const)


def trig(where, freq, nodes, cen):
    n = 10 * COLS * K
    return pl.pallas_call(
        trig_kernel,
        out_shape=[jax.ShapeDtypeStruct((10, COLS, K), F32)] * 2,
        in_specs=[pl.BlockSpec(memory_space=pltpu.SMEM)]
        + [pl.BlockSpec(memory_space=pltpu.VMEM)] * 3,
        out_specs=[pl.BlockSpec(memory_space=pltpu.VMEM)] * 2,
        scratch_shapes=[pltpu.VMEM((2, COLS, 10), F32), pltpu.VMEM((2, COLS, 24), F32)],
        compiler_params=pltpu.CompilerParams(vmem_limit_bytes=24 * 2**20),
        cost_estimate=pl.CostEstimate(flops=n * 40, bytes_accessed=n * 8, transcendentals=0),
        name="trig",
    )(where, freq, nodes, cen)


def main_kernel(
    where_ref, field_ref, cos_ref, sin_ref, interp_ref, eval_ref, out_ref, low_ref, high_ref, s_ref
):
    half = where_ref[1]
    nt = (((1,), (1,)), ((), ()))

    def dot(a, b):
        return lax.dot_general(a, b, nt, preferred_element_type=F32)

    def rotated(index, here, re, im):
        c, s = cos_ref[index, here, :], sin_ref[index, here, :]
        return c * re - s * im, s * re + c * im

    for level in range(3):
        for q in range(8):
            here = slice(q * 16, q * 16 + 16)
            for kind, w_ref in enumerate((low_ref, high_ref)):
                src = (q & ~(1 << level)) | (kind << level)
                there = slice(src * 16, src * 16 + 16)
                if level == 0:
                    re = field_ref[there, :K].astype(F32)
                    im = field_ref[there, K:].astype(F32)
                else:
                    re = s_ref[src * 16 : src * 16 + 16, :]
                    im = s_ref[COLS + src * 16 : COLS + src * 16 + 16, :]
                re, im = rotated(2 * level + kind, here, re, im)
                w_ref[q * 16 : q * 16 + 16, :] = re.astype(BF16)
                w_ref[COLS + q * 16 : COLS + q * 16 + 16, :] = im.astype(BF16)
        s_ref[...] = dot(low_ref[...], interp_ref[0]) + dot(high_ref[...], interp_ref[1])

    for t, w_ref in enumerate((low_ref, high_ref)):
        for q in range(8):
            here = slice(q * 16, q * 16 + 16)
            re, im = rotated(6 + t, here, s_ref[here, :], s_ref[COLS + q * 16 : COLS + q * 16 + 16, :])
            w_ref[q * 16 : q * 16 + 16, :] = re.astype(BF16)
            w_ref[COLS + q * 16 : COLS + q * 16 + 16, :] = im.astype(BF16)

    a = lax.broadcasted_iota(jnp.int32, (32, COLS), 0)
    b = lax.broadcasted_iota(jnp.int32, (32, COLS), 1)
    gather = jnp.where((a // 4 == b // 16) & (a % 4 == b % 4), 1.0, 0.0).astype(BF16)
    mine = interp_ref[half]
    for t, w_ref in enumerate((low_ref, high_ref)):
        s_ref[...] = dot(w_ref[...], mine)
        for q in range(8):
            here = slice(q * 16, q * 16 + 16)
            c, s = cos_ref[8 + t, here, :], sin_ref[8 + t, here, :]
            v = c * s_ref[here, :] - s * s_ref[COLS + q * 16 : COLS + q * 16 + 16, :]
            w_ref[here, :] = v.astype(BF16)
        v = jnp.dot(gather, w_ref[:COLS, :], preferred_element_type=F32).astype(BF16)
        out_ref[t * 32 : t * 32 + 32, :] = dot(v, eval_ref[...]).astype(BF16)


def levels(where, field, cosine, sine, interp, evaluate):
    vmem = pl.BlockSpec(memory_space=pltpu.VMEM)
    return pl.pallas_call(
        main_kernel,
        out_shape=jax.ShapeDtypeStruct((64, PIX), BF16),
        in_specs=[pl.BlockSpec(memory_space=pltpu.SMEM)] + [vmem] * 5,
        out_specs=vmem,
        scratch_shapes=[
            pltpu.VMEM((2 * COLS, K), BF16),
            pltpu.VMEM((2 * COLS, K), BF16),
            pltpu.VMEM((2 * COLS, K), F32),
        ],
        compiler_params=pltpu.CompilerParams(vmem_limit_bytes=32 * 2**20),
        cost_estimate=pl.CostEstimate(
            flops=8 * 2 * K * K * 256, bytes_accessed=10 * 2**20, transcendentals=0
        ),
        name="levels",
    )(where, field, cosine, sine, interp, evaluate)


def exchange(block, axes):
    return lax.all_to_all(block, axes, split_axis=0, concat_axis=0, tiled=True)


def body(coeffs, freqs, nodes, centres, interp, evaluate):
    where = jnp.stack([lax.axis_index("y"), lax.axis_index("z4")]).astype(jnp.int32)
    field = jnp.transpose(coeffs[0], (2, 1, 0)).reshape(32, 4, 2 * K)
    freq = jnp.transpose(freqs[0], (2, 0, 1)).reshape(1, 32, 4, 10)
    freq = jnp.broadcast_to(freq, (2, 32, 4, 10)).reshape(64, 1, 40)
    freq = exchange(freq, FAR).reshape(2, COLS, 10)
    field = exchange(field, NEAR).reshape(COLS, 2 * K)
    cosine, sine = trig(where, freq, nodes.reshape(24, K), centres.reshape(24, 64))
    part = levels(where, field, cosine, sine, interp, evaluate)
    part = part.reshape(16, 4, 8, 128).transpose(0, 2, 1, 3).reshape(128, 4, 128)
    part = exchange(part, ALL)
    total = jnp.sum(part.reshape(2, 8, 2, 4, 4, 128).astype(F32), axis=(0, 2))
    return total.reshape(COLS, 128).T


def solution(mesh):
    fine = Mesh(mesh.devices.reshape(SIZES), AXES)
    box, ang = ("y", "z4", "z2", "z1", "c"), ("zh", "x")
    return jax.shard_map(
        body,
        mesh=fine,
        in_specs=(P(ang, None, None, box), P(ang, None, None, box), P(), P(), P(), P()),
        out_specs=P(ang, box),
        check_vma=False,
    )
```

```python
import jax
import jax.numpy as jnp
import numpy as np
from jax import lax
from jax.experimental import pallas as pl
from jax.experimental.pallas import tpu as pltpu
from jax.sharding import Mesh, PartitionSpec as P

AXES = ("y", "z4", "z2", "z1", "c", "zh", "x")
SIZES = (4, 2, 2, 2, 2, 2, 4)
NEAR = ("z2", "z1", "c", "x")
ALL = ("z4", "z2", "z1", "c", "zh", "x")
K = 576
WIDE = 1280
COLS = 128
PIX = 1024
F32 = jnp.float32
BF16 = jnp.bfloat16
HIGHEST = lax.Precision.HIGHEST
VMEM = pl.BlockSpec(memory_space=pltpu.VMEM)
HBM = pl.BlockSpec(memory_space=pltpu.HBM)

COS = (
    0.999999989059023,
    -19.739204499453944,
    64.9391174598965,
    -85.45013953089278,
    60.16763095097771,
    -25.96759924841038,
    6.5286581610231424,
)
SIN = (
    6.283184916495431,
    -41.34158923268858,
    81.59994332978287,
    -76.61447253124996,
    41.34288235456833,
    -12.471243535026977,
)

OWN, LOW1, HIGH1, LOW2, HIGH2, ACROSS = range(6)
FREQS = []


def lanes_of(rows, level):
    FREQS.extend((rows, level, d) for d in range(2))
    return len(FREQS) - 2


F0, F1, F2, F3, F4 = (lanes_of(OWN, level) for level in range(5))
UP1 = lanes_of(LOW1, 0), lanes_of(HIGH1, 0)
UP2 = lanes_of(LOW2, 1), lanes_of(HIGH2, 1)
A3, A4 = (lanes_of(ACROSS, level) for level in (3, 4))

SETS = [
    [(-1, F0, 0, 0)],
    [(-1, F0, 0, 1)],
    [(1, UP1[0], 0, 2), (-1, F1, 1, 0)],
    [(1, UP1[1], 0, 2), (-1, F1, 1, 1)],
    [(1, UP2[0], 1, 2), (-1, F2, 2, 0)],
    [(1, UP2[1], 1, 2), (-1, F2, 2, 1)],
    [(1, F2, 2, 2), (-1, F3, 3, None)],
    [(1, F3, 3, 2), (1, F4, 3, 2)],
    [(1, F2, 2, 2), (-1, A3, 3, None)],
    [(1, A3, 3, 2), (1, A4, 3, 2)],
]
HERE = 8
TERMS = [
    (s, sign, lane + d, level, kind, d)
    for s, terms in enumerate(SETS)
    for sign, lane, level, kind in terms
    for d in range(2)
]


def tables():
    pick = np.zeros((6, 16, 256), np.float32)
    for lane, (rows, level, d) in enumerate(FREQS):
        at = level * 2 + d
        for piece in range(3):
            pick[rows, at, 32 * piece + lane] = 1
        for i, term in enumerate(TERMS):
            if term[2] == lane:
                pick[rows, at, 128 + i] = 1
    centre = np.zeros((2, 24, 128), np.float32)
    mask = np.zeros((8, 128), np.float32)
    for i, (s, sign, lane, level, kind, d) in enumerate(TERMS):
        for half in range(2):
            k = half if kind is None else kind
            centre[half, (level * 3 + k) * 2 + d, i] = sign
        mask[FREQS[lane][0], i] = 1
    return pick, centre, mask


PICK, CENTRE, MASK = tables()


def moved(q, rows):
    return {OWN: q, LOW1: q & ~2, HIGH1: q | 2, LOW2: q & ~4, HIGH2: q | 4}[rows]


def prepare_kernel(
    nodes_ref, cen_ref, centre_ref, mask_ref, pick_ref, b_ref, c_ref, pick_out_ref, wide_ref
):
    pick_out_ref[...] = pick_ref[...]
    base = lax.axis_index("y") * 16
    half = lax.axis_index("z4")
    turn = 0.5 / np.pi
    wide_ref[...] = jnp.zeros_like(wide_ref)
    for s, sign, lane, level, kind, d in TERMS:

        def row(kind):
            i = (level * 3 + kind) * 2 + d
            return nodes_ref[i : i + 1, :]

        value = jnp.where(half == 0, row(0), row(1)) if kind is None else row(kind)
        wide_ref[s, lane : lane + 1, :] = value * (sign * turn)
    for s in range(len(SETS)):
        rest = wide_ref[s]
        for piece in range(3):
            part = rest.astype(BF16)
            b_ref[s, 32 * piece : 32 * piece + 32, :] = part
            rest = rest - part.astype(F32)
        b_ref[s, 96:128, :] = jnp.zeros((32, K), BF16)

    picked = lax.dot_general(
        cen_ref[...] * turn,
        centre_ref[half],
        (((0,), (0,)), ((), ())),
        precision=HIGHEST,
        preferred_element_type=F32,
    )
    q = lax.broadcasted_iota(jnp.int32, (COLS, 64), 0) // 16
    lane = lax.broadcasted_iota(jnp.int32, (COLS, 64), 1)
    own = base + half * 8
    across = base + 8 - half * 8
    boxes = [own + q, own + (q & ~2), own + (q | 2), own + (q & ~4), own + (q | 4), across + q]
    total = jnp.zeros((COLS, 128), F32)
    for v, box in enumerate(boxes):
        hot = jnp.where(lane == box, 1.0, 0.0).astype(F32)
        mine = jnp.dot(hot, picked, precision=HIGHEST, preferred_element_type=F32)
        total = total + mine * mask_ref[v : v + 1, :]
    c_ref[...] = total


def prepare(nodes, cen):
    return pl.pallas_call(
        prepare_kernel,
        out_shape=[
            jax.ShapeDtypeStruct((10, 128, K), BF16),
            jax.ShapeDtypeStruct((COLS, 128), F32),
            jax.ShapeDtypeStruct(PICK.shape, BF16),
        ],
        in_specs=[VMEM] * 5,
        out_specs=[VMEM] * 3,
        scratch_shapes=[pltpu.VMEM((10, 32, K), F32)],
        compiler_params=pltpu.CompilerParams(vmem_limit_bytes=6 * 2**20),
        cost_estimate=pl.CostEstimate(flops=10**7, bytes_accessed=5 * 2**20, transcendentals=0),
        name="prepare",
    )(nodes, cen, jnp.asarray(CENTRE), jnp.asarray(MASK), jnp.asarray(PICK, BF16))


def pack_kernel(coeffs_ref, freqs_ref, out_ref):
    def spread(rows):
        i = lax.broadcasted_iota(jnp.int32, (rows, rows), 0)
        j = lax.broadcasted_iota(jnp.int32, (rows, rows), 1)
        half = rows // 2
        return jnp.where(i == 2 * (j % half) + j // half, 1.0, 0.0).astype(BF16)

    def turned(x, y):
        z = lax.dot_general(x, y, (((0,), (0,)), ((), ())), preferred_element_type=F32)
        return z.reshape(32, 4, z.shape[1]).astype(BF16)

    whole, tail = spread(256), spread(128)
    for m in range(4):
        z = turned(coeffs_ref[m * 256 : m * 256 + 256, :], whole)
        out_ref[:, :, m * 128 : m * 128 + 128] = z[:, :, :128]
        out_ref[:, :, 512 + m * 128 : 512 + m * 128 + 128] = z[:, :, 128:]
    out_ref[:, :, 1024:1152] = turned(coeffs_ref[1024:1152, :], tail)
    i = lax.broadcasted_iota(jnp.int32, (10, 128), 0)
    j = lax.broadcasted_iota(jnp.int32, (10, 128), 1)
    out_ref[:, :, 1152:] = turned(freqs_ref[...], jnp.where(i == j, 1.0, 0.0).astype(BF16))


def pack(coeffs, freqs):
    return pl.pallas_call(
        pack_kernel,
        out_shape=jax.ShapeDtypeStruct((32, 4, WIDE), BF16),
        in_specs=[VMEM] * 2,
        out_specs=VMEM,
        compiler_params=pltpu.CompilerParams(vmem_limit_bytes=4 * 2**20),
        cost_estimate=pl.CostEstimate(flops=10**7, bytes_accessed=2**20, transcendentals=0),
        name="pack",
    )(coeffs, freqs)


def horner(coefficients, u):
    total = u * coefficients[-1] + coefficients[-2]
    for value in coefficients[-3::-1]:
        total = total * u + value
    return total


def cos_sin(turns):
    r = turns - jnp.floor(turns + 0.5)
    u = r * r
    return horner(COS, u), r * horner(SIN, u)


def dot(a, b):
    return lax.dot_general(a, b, (((1,), (1,)), ((), ())), preferred_element_type=F32)


def block(q):
    return slice(q * 16, q * 16 + 16)


def phases(placed, b_ref, c_ref, sets, t_ref):
    lanes = placed[:, :128].astype(BF16)
    i = lax.broadcasted_iota(jnp.int32, (128, 128), 0)
    j = lax.broadcasted_iota(jnp.int32, (128, 128), 1)
    first = jnp.where(i < 4, i // 2, (i - 4) // 4 + 2)
    gather = jnp.where((first == j) & (i < len(TERMS)), 1.0, 0.0).astype(F32)
    const = jnp.dot(placed[:, 128:] * c_ref[...], gather, precision=HIGHEST, preferred_element_type=F32)
    for i, s in enumerate(sets):
        t_ref[i] = jnp.dot(lanes, b_ref[s], preferred_element_type=F32) + const[:, s : s + 1]


def rotated(turns, re, im):
    c, s = cos_sin(turns)
    return c * re - s * im, s * re + c * im


def contribution(state_ref, turns_ref, first, mine, fetch, evaluate_ref, w_ref, s_ref):
    for q in range(8):
        here = block(q)
        re, im = rotated(turns_ref[first, here, :], state_ref[here, :], state_ref[block(q + 8), :])
        w_ref[here, :] = re.astype(BF16)
        w_ref[block(q + 8), :] = im.astype(BF16)
    s_ref[...] = dot(w_ref[...], mine)
    for q in range(8):
        here = block(q)
        c, s = cos_sin(turns_ref[first + 1, here, :])
        v = c * s_ref[here, :] - s * s_ref[block(q + 8), :]
        w_ref[here, :] = v.astype(BF16)
    a = lax.broadcasted_iota(jnp.int32, (32, COLS), 0)
    b = lax.broadcasted_iota(jnp.int32, (32, COLS), 1)
    angles = jnp.where((a // 4 == b // 16) & (a % 4 == b % 4), 1.0, 0.0).astype(BF16)
    v = jnp.dot(angles, w_ref[:COLS, :], preferred_element_type=F32).astype(BF16)
    fetch.wait()
    return jnp.dot(v, evaluate_ref[...], preferred_element_type=F32).astype(BF16)


def fields(field_ref, q):
    x = field_ref[4 * q : 4 * q + 4].astype(F32).reshape(16, WIDE)
    re = jnp.concatenate([x[:, :512], x[:, 1024:1088]], axis=1)
    im = jnp.concatenate([x[:, 512:1024], x[:, 1088:1152]], axis=1)
    return re, im


def own_kernel(
    field_ref,
    freq_ref,
    b_ref,
    c_ref,
    pick_ref,
    interp_ref,
    eval_ref,
    out_ref,
    s_ref,
    low_ref,
    high_ref,
    last_ref,
    t_ref,
    evaluate_ref,
    sem,
):
    fetch = pltpu.make_async_copy(eval_ref, evaluate_ref, sem)
    fetch.start()
    freq = freq_ref[...].astype(F32).reshape(COLS, 128)[:, :16].astype(BF16)
    placed = jnp.zeros((COLS, 256), F32)
    for rows in range(ACROSS):
        source = jnp.concatenate([freq[block(moved(q, rows))] for q in range(8)], axis=0)
        placed = placed + jnp.dot(source, pick_ref[rows], preferred_element_type=F32)
    phases(placed, b_ref, c_ref, range(HERE), t_ref)

    for level in range(3):
        for q in range(8):
            here = block(q)
            for kind, w_ref in enumerate((low_ref, high_ref)):
                src = (q & ~(1 << level)) | (kind << level)
                if level == 0:
                    re, im = fields(field_ref, src)
                else:
                    re = s_ref[block(src), :]
                    im = s_ref[block(src + 8), :]
                re, im = rotated(t_ref[2 * level + kind, here, :], re, im)
                w_ref[here, :] = re.astype(BF16)
                w_ref[block(q + 8), :] = im.astype(BF16)
        s_ref[...] = dot(low_ref[...], interp_ref[0]) + dot(high_ref[...], interp_ref[1])
    mine = interp_ref[lax.axis_index("z4")]
    out_ref[...] = contribution(s_ref, t_ref, 6, mine, fetch, evaluate_ref, low_ref, last_ref)


def across_kernel(
    freq_ref,
    freq_across_ref,
    own_ref,
    s_ref,
    b_ref,
    c_ref,
    pick_ref,
    interp_ref,
    eval_ref,
    out_ref,
    w_ref,
    last_ref,
    t_ref,
    evaluate_ref,
    sem,
):
    fetch = pltpu.make_async_copy(eval_ref, evaluate_ref, sem)
    fetch.start()
    half = lax.axis_index("z4")
    placed = jnp.zeros((COLS, 256), F32)
    for rows, ref in ((OWN, freq_ref), (ACROSS, freq_across_ref)):
        freq = ref[...].astype(F32).reshape(COLS, 128)[:, :16].astype(BF16)
        placed = placed + jnp.dot(freq, pick_ref[rows], preferred_element_type=F32)
    phases(placed, b_ref, c_ref, (HERE, HERE + 1), t_ref)
    part = contribution(s_ref, t_ref, 0, interp_ref[half], fetch, evaluate_ref, w_ref, last_ref)
    out_ref[half] = own_ref[...]
    out_ref[1 - half] = part


def own_levels(field, freq, tables, interp, evaluate):
    return pl.pallas_call(
        own_kernel,
        out_shape=[
            jax.ShapeDtypeStruct((32, PIX), BF16),
            jax.ShapeDtypeStruct((2 * COLS, K), F32),
        ],
        in_specs=[VMEM] * 6 + [HBM],
        out_specs=[VMEM] * 2,
        scratch_shapes=[
            pltpu.VMEM((2 * COLS, K), BF16),
            pltpu.VMEM((2 * COLS, K), BF16),
            pltpu.VMEM((2 * COLS, K), F32),
            pltpu.VMEM((HERE, COLS, K), F32),
            pltpu.VMEM((K, PIX), BF16),
            pltpu.SemaphoreType.DMA,
        ],
        compiler_params=pltpu.CompilerParams(vmem_limit_bytes=12 * 2**20),
        cost_estimate=pl.CostEstimate(
            flops=8 * 2 * K * K * 256, bytes_accessed=10 * 2**20, transcendentals=0
        ),
        name="own_levels",
    )(field, freq, *tables, interp, evaluate)


def across_level(freq, freq_across, own, state, tables, interp, evaluate):
    return pl.pallas_call(
        across_kernel,
        out_shape=jax.ShapeDtypeStruct((2, 32, PIX), BF16),
        in_specs=[VMEM] * 8 + [HBM],
        out_specs=VMEM,
        scratch_shapes=[
            pltpu.VMEM((2 * COLS, K), BF16),
            pltpu.VMEM((2 * COLS, K), F32),
            pltpu.VMEM((2, COLS, K), F32),
            pltpu.VMEM((K, PIX), BF16),
            pltpu.SemaphoreType.DMA,
        ],
        compiler_params=pltpu.CompilerParams(vmem_limit_bytes=12 * 2**20),
        cost_estimate=pl.CostEstimate(
            flops=2 * 2 * K * K * 256, bytes_accessed=5 * 2**20, transcendentals=0
        ),
        name="across_level",
    )(freq, freq_across, own, state, *tables, interp, evaluate)


def exchange(block, axes):
    return lax.all_to_all(block, axes, split_axis=0, concat_axis=0, tiled=True)


def body(coeffs, freqs, nodes, centres, interp, evaluate):
    field = exchange(pack(coeffs.reshape(2 * K, COLS), freqs.reshape(10, COLS)), NEAR)
    freq = field[:, :, WIDE - 128 :]
    freq_across = lax.ppermute(freq, "z4", [(0, 1), (1, 0)])
    tables = prepare(nodes.reshape(24, K), centres.reshape(24, 64))
    own, state = own_levels(field, freq, tables, interp, evaluate.T)
    part = across_level(freq, freq_across, own, state, tables, interp, evaluate.T)
    part = part.reshape(16, 4, 8, 128).transpose(0, 2, 1, 3).reshape(128, 4, 128)
    part = exchange(part, ALL)
    total = jnp.sum(part.reshape(2, 8, 2, 4, 4, 128).astype(F32), axis=(0, 2))
    return total.reshape(COLS, 128).T


def solution(mesh):
    fine = Mesh(mesh.devices.reshape(SIZES), AXES)
    box, ang = ("y", "z4", "z2", "z1", "c"), ("zh", "x")
    return jax.shard_map(
        body,
        mesh=fine,
        in_specs=(P(ang, None, None, box), P(ang, None, None, box), P(), P(), P(), P()),
        out_specs=P(ang, box),
        check_vma=False,
    )
```

```python
import jax
import jax.numpy as jnp
import numpy as np
from jax import lax
from jax.experimental import pallas as pl
from jax.experimental.pallas import tpu as pltpu
from jax.sharding import Mesh, PartitionSpec as P

AXES = ("y", "z4", "z2", "z1", "c", "zh", "x")
SIZES = (4, 2, 2, 2, 2, 2, 4)
NEAR = ("z2", "z1", "c", "x")
ALL = ("z4", "z2", "z1", "c", "zh", "x")
K = 576
WIDE = 1280
COLS = 128
PIX = 1024
F32 = jnp.float32
BF16 = jnp.bfloat16
HIGHEST = lax.Precision.HIGHEST
VMEM = pl.BlockSpec(memory_space=pltpu.VMEM)

COS = (
    0.999999989059023,
    -19.739204499453944,
    64.9391174598965,
    -85.45013953089278,
    60.16763095097771,
    -25.96759924841038,
    6.5286581610231424,
)
SIN = (
    6.283184916495431,
    -41.34158923268858,
    81.59994332978287,
    -76.61447253124996,
    41.34288235456833,
    -12.471243535026977,
)

OWN, LOW1, HIGH1, LOW2, HIGH2, ACROSS = range(6)
FREQS = []


def lanes_of(rows, level):
    FREQS.extend((rows, level, d) for d in range(2))
    return len(FREQS) - 2


F0, F1, F2, F3, F4 = (lanes_of(OWN, level) for level in range(5))
UP1 = lanes_of(LOW1, 0), lanes_of(HIGH1, 0)
UP2 = lanes_of(LOW2, 1), lanes_of(HIGH2, 1)
A3, A4 = (lanes_of(ACROSS, level) for level in (3, 4))

SETS = [
    [(-1, F0, 0, 0)],
    [(-1, F0, 0, 1)],
    [(1, UP1[0], 0, 2), (-1, F1, 1, 0)],
    [(1, UP1[1], 0, 2), (-1, F1, 1, 1)],
    [(1, UP2[0], 1, 2), (-1, F2, 2, 0)],
    [(1, UP2[1], 1, 2), (-1, F2, 2, 1)],
    [(1, F2, 2, 2), (-1, F3, 3, None)],
    [(1, F3, 3, 2), (1, F4, 3, 2)],
    [(1, F2, 2, 2), (-1, A3, 3, None)],
    [(1, A3, 3, 2), (1, A4, 3, 2)],
]
HERE = 8
TERMS = [
    (s, sign, lane + d, level, kind, d)
    for s, terms in enumerate(SETS)
    for sign, lane, level, kind in terms
    for d in range(2)
]


def tables():
    pick = np.zeros((6, 16, 256), np.float32)
    for lane, (rows, level, d) in enumerate(FREQS):
        at = level * 2 + d
        for piece in range(3):
            pick[rows, at, 32 * piece + lane] = 1
        for i, term in enumerate(TERMS):
            if term[2] == lane:
                pick[rows, at, 128 + i] = 1
    centre = np.zeros((2, 24, 128), np.float32)
    mask = np.zeros((8, 128), np.float32)
    for i, (s, sign, lane, level, kind, d) in enumerate(TERMS):
        for half in range(2):
            k = half if kind is None else kind
            centre[half, (level * 3 + k) * 2 + d, i] = sign
        mask[FREQS[lane][0], i] = 1
    return pick, centre, mask


PICK, CENTRE, MASK = tables()


def moved(q, rows):
    return {OWN: q, LOW1: q & ~2, HIGH1: q | 2, LOW2: q & ~4, HIGH2: q | 4}[rows]


def prepare_kernel(nodes_ref, cen_ref, centre_ref, mask_ref, pick_ref, out_ref, wide_ref):
    base = lax.axis_index("y") * 16
    half = lax.axis_index("z4")
    turn = 0.5 / np.pi

    def pieces(rest):
        for piece in range(3):
            part = rest.astype(BF16)
            yield piece, part
            rest = rest - part.astype(F32)

    wide_ref[...] = jnp.zeros_like(wide_ref)
    for s, sign, lane, level, kind, d in TERMS:

        def row(kind):
            i = (level * 3 + kind) * 2 + d
            return nodes_ref[i : i + 1, :]

        value = jnp.where(half == 0, row(0), row(1)) if kind is None else row(kind)
        wide_ref[s, lane : lane + 1, :] = value * (sign * turn)
    for s in range(len(SETS)):
        for piece, part in pieces(wide_ref[s]):
            out_ref[s, 32 * piece : 32 * piece + 32, :] = part

    picked = lax.dot_general(
        cen_ref[...] * turn,
        centre_ref[half],
        (((0,), (0,)), ((), ())),
        precision=HIGHEST,
        preferred_element_type=F32,
    )
    q = lax.broadcasted_iota(jnp.int32, (32, 64), 0) & 7
    lane = lax.broadcasted_iota(jnp.int32, (32, 64), 1)
    own = base + half * 8
    across = base + 8 - half * 8
    boxes = [own + q, own + (q & ~2), own + (q | 2), own + (q & ~4), own + (q | 4), across + q]
    total = jnp.zeros((32, 128), F32)
    for v, box in enumerate(boxes):
        hot = jnp.where(lane == box, 1.0, 0.0).astype(F32)
        mine = jnp.dot(hot, picked, precision=HIGHEST, preferred_element_type=F32)
        total = total + mine * mask_ref[v : v + 1, :]
    for piece, part in pieces(total):
        out_ref[10, 32 * piece : 32 * piece + 32, :128] = part
    out_ref[11, :, :256] = pick_ref[...]


def prepare(nodes, cen):
    return pl.pallas_call(
        prepare_kernel,
        out_shape=jax.ShapeDtypeStruct((12, 96, K), BF16),
        in_specs=[VMEM] * 5,
        out_specs=VMEM,
        scratch_shapes=[pltpu.VMEM((10, 32, K), F32)],
        compiler_params=pltpu.CompilerParams(vmem_limit_bytes=6 * 2**20),
        cost_estimate=pl.CostEstimate(flops=10**7, bytes_accessed=5 * 2**20, transcendentals=0),
        name="prepare",
    )(nodes, cen, jnp.asarray(CENTRE), jnp.asarray(MASK), jnp.asarray(PICK.reshape(96, 256), BF16))


def pack_kernel(coeffs_ref, freqs_ref, out_ref):
    def spread(rows):
        i = lax.broadcasted_iota(jnp.int32, (rows, rows), 0)
        j = lax.broadcasted_iota(jnp.int32, (rows, rows), 1)
        half = rows // 2
        return jnp.where(i == 2 * (j % half) + j // half, 1.0, 0.0).astype(BF16)

    def turned(x, y):
        z = lax.dot_general(x, y, (((0,), (0,)), ((), ())), preferred_element_type=F32)
        return z.reshape(32, 4, z.shape[1]).astype(BF16)

    whole, tail = spread(256), spread(128)
    for m in range(4):
        z = turned(coeffs_ref[m * 256 : m * 256 + 256, :], whole)
        out_ref[:, :, m * 128 : m * 128 + 128] = z[:, :, :128]
        out_ref[:, :, 512 + m * 128 : 512 + m * 128 + 128] = z[:, :, 128:]
    out_ref[:, :, 1024:1152] = turned(coeffs_ref[1024:1152, :], tail)
    i = lax.broadcasted_iota(jnp.int32, (10, 128), 0)
    j = lax.broadcasted_iota(jnp.int32, (10, 128), 1)
    out_ref[:, :, 1152:] = turned(freqs_ref[...].astype(F32).reshape(10, COLS).astype(BF16), jnp.where(i == j, 1.0, 0.0).astype(BF16))


def pack(coeffs, freqs):
    return pl.pallas_call(
        pack_kernel,
        out_shape=jax.ShapeDtypeStruct((32, 4, WIDE), BF16),
        in_specs=[VMEM] * 2,
        out_specs=VMEM,
        compiler_params=pltpu.CompilerParams(vmem_limit_bytes=4 * 2**20),
        cost_estimate=pl.CostEstimate(flops=10**7, bytes_accessed=2**20, transcendentals=0),
        name="pack",
    )(coeffs, freqs)


def horner(coefficients, u):
    total = u * coefficients[-1] + coefficients[-2]
    for value in coefficients[-3::-1]:
        total = total * u + value
    return total


def cos_sin(turns):
    r = turns - jnp.floor(turns + 0.5)
    u = r * r
    return horner(COS, u), r * horner(SIN, u)


def dot(a, b):
    return lax.dot_general(a, b, (((1,), (1,)), ((), ())), preferred_element_type=F32)


def block(q):
    return slice(q * 16, q * 16 + 16)


def picked(table_ref, rows, freq):
    pick = table_ref[11, 16 * rows : 16 * rows + 16, :256]
    return jnp.dot(freq, pick, preferred_element_type=F32)


def phases(placed, table_ref, sets, t_ref):
    lanes = placed[:, :96].astype(BF16)
    i = lax.broadcasted_iota(jnp.int32, (128, 128), 0)
    j = lax.broadcasted_iota(jnp.int32, (128, 128), 1)
    first = jnp.where(i < 4, i // 2, (i - 4) // 4 + 2)
    gather = jnp.where((first == j) & (i < len(TERMS)), 1.0, 0.0).astype(F32)
    high, mid, low = (table_ref[10, 32 * p : 32 * p + 32, :128].astype(F32) for p in range(3))
    centre = high + mid + low
    centre = jnp.concatenate(
        [jnp.broadcast_to(centre[q : q + 1], (16, 128)) for q in range(8)], axis=0
    )
    const = jnp.dot(placed[:, 128:] * centre, gather, precision=HIGHEST, preferred_element_type=F32)
    for i, s in enumerate(sets):
        t_ref[i] = jnp.dot(lanes, table_ref[s], preferred_element_type=F32) + const[:, s : s + 1]


def rotated(turns, re, im):
    c, s = cos_sin(turns)
    return c * re - s * im, s * re + c * im


def contribution(state_ref, turns_ref, first, mine, w_ref, s_ref):
    for q in range(8):
        here = block(q)
        re, im = rotated(turns_ref[first, here, :], state_ref[here, :], state_ref[block(q + 8), :])
        w_ref[here, :] = re.astype(BF16)
        w_ref[block(q + 8), :] = im.astype(BF16)
    s_ref[...] = dot(w_ref[...], mine)
    for q in range(8):
        here = block(q)
        c, s = cos_sin(turns_ref[first + 1, here, :])
        v = c * s_ref[here, :] - s * s_ref[block(q + 8), :]
        w_ref[here, :] = v.astype(BF16)
    a = lax.broadcasted_iota(jnp.int32, (32, COLS), 0)
    b = lax.broadcasted_iota(jnp.int32, (32, COLS), 1)
    angles = jnp.where((a // 4 == b // 16) & (a % 4 == b % 4), 1.0, 0.0).astype(BF16)
    return jnp.dot(angles, w_ref[:COLS, :], preferred_element_type=F32).astype(BF16)


def fields(field_ref, q):
    x = field_ref[4 * q : 4 * q + 4].astype(F32).reshape(16, WIDE)
    re = jnp.concatenate([x[:, :512], x[:, 1024:1088]], axis=1)
    im = jnp.concatenate([x[:, 512:1024], x[:, 1088:1152]], axis=1)
    return re, im


def lanes_16(freq_ref):
    return freq_ref[...].astype(F32).reshape(COLS, 128)[:, :16].astype(BF16)


def own_kernel(
    field_ref, freq_ref, table_ref, interp_ref, v_ref, s_ref, low_ref, high_ref, last_ref, t_ref
):
    freq = lanes_16(freq_ref)
    placed = jnp.zeros((COLS, 256), F32)
    for rows in range(ACROSS):
        source = jnp.concatenate([freq[block(moved(q, rows))] for q in range(8)], axis=0)
        placed = placed + picked(table_ref, rows, source)
    phases(placed, table_ref, range(HERE), t_ref)

    for level in range(3):
        for q in range(8):
            here = block(q)
            for kind, w_ref in enumerate((low_ref, high_ref)):
                src = (q & ~(1 << level)) | (kind << level)
                if level == 0:
                    re, im = fields(field_ref, src)
                else:
                    re = s_ref[block(src), :]
                    im = s_ref[block(src + 8), :]
                re, im = rotated(t_ref[2 * level + kind, here, :], re, im)
                w_ref[here, :] = re.astype(BF16)
                w_ref[block(q + 8), :] = im.astype(BF16)
        s_ref[...] = dot(low_ref[...], interp_ref[0]) + dot(high_ref[...], interp_ref[1])
    mine = interp_ref[lax.axis_index("z4")]
    v_ref[...] = contribution(s_ref, t_ref, 6, mine, low_ref, last_ref)


def across_kernel(
    freq_ref,
    freq_across_ref,
    v_ref,
    s_ref,
    table_ref,
    interp_ref,
    eval_ref,
    out_ref,
    w_ref,
    last_ref,
    t_ref,
):
    half = lax.axis_index("z4")
    placed = picked(table_ref, OWN, lanes_16(freq_ref))
    placed = placed + picked(table_ref, ACROSS, lanes_16(freq_across_ref))
    phases(placed, table_ref, (HERE, HERE + 1), t_ref)
    v = contribution(s_ref, t_ref, 0, interp_ref[half], w_ref, last_ref)
    for where, value in ((half, v_ref[...]), (1 - half, v)):
        part = jnp.dot(value, eval_ref[...], preferred_element_type=F32)
        out_ref[where] = part.astype(BF16)


def own_levels(field, freq, table, interp):
    return pl.pallas_call(
        own_kernel,
        out_shape=[
            jax.ShapeDtypeStruct((32, K), BF16),
            jax.ShapeDtypeStruct((2 * COLS, K), F32),
        ],
        in_specs=[VMEM] * 4,
        out_specs=[VMEM] * 2,
        scratch_shapes=[
            pltpu.VMEM((2 * COLS, K), BF16),
            pltpu.VMEM((2 * COLS, K), BF16),
            pltpu.VMEM((2 * COLS, K), F32),
            pltpu.VMEM((HERE, COLS, K), F32),
        ],
        compiler_params=pltpu.CompilerParams(vmem_limit_bytes=8 * 2**20),
        cost_estimate=pl.CostEstimate(
            flops=8 * 2 * K * K * 256, bytes_accessed=10 * 2**20, transcendentals=0
        ),
        name="own_levels",
    )(field, freq, table, interp)


def across_level(freq, freq_across, v, state, table, interp, evaluate):
    return pl.pallas_call(
        across_kernel,
        out_shape=jax.ShapeDtypeStruct((2, 32, PIX), BF16),
        in_specs=[VMEM] * 7,
        out_specs=VMEM,
        scratch_shapes=[
            pltpu.VMEM((2 * COLS, K), BF16),
            pltpu.VMEM((2 * COLS, K), F32),
            pltpu.VMEM((2, COLS, K), F32),
        ],
        compiler_params=pltpu.CompilerParams(vmem_limit_bytes=6 * 2**20),
        cost_estimate=pl.CostEstimate(
            flops=2 * 2 * K * K * 256, bytes_accessed=5 * 2**20, transcendentals=0
        ),
        name="across_level",
    )(freq, freq_across, v, state, table, interp, evaluate)


def exchange(block, axes):
    return lax.all_to_all(block, axes, split_axis=0, concat_axis=0, tiled=True)


def body(coeffs, freqs, nodes, centres, interp, evaluate):
    field = exchange(pack(coeffs.reshape(2 * K, COLS), freqs[0]), NEAR)
    freq = field[:, :, WIDE - 128 :]
    freq_across = lax.ppermute(freq, "z4", [(0, 1), (1, 0)])
    table = prepare(nodes.reshape(24, K), centres.reshape(24, 64))
    v, state = own_levels(field, freq, table, interp)
    part = across_level(freq, freq_across, v, state, table, interp, evaluate.T)
    part = part.reshape(16, 4, 8, 128).transpose(0, 2, 1, 3).reshape(128, 4, 128)
    part = exchange(part, ALL)
    total = jnp.sum(part.reshape(2, 8, 2, 4, 4, 128).astype(F32), axis=(0, 2))
    return total.reshape(COLS, 128).T


def solution(mesh):
    fine = Mesh(mesh.devices.reshape(SIZES), AXES)
    box, ang = ("y", "z4", "z2", "z1", "c"), ("zh", "x")
    return jax.shard_map(
        body,
        mesh=fine,
        in_specs=(P(ang, None, None, box), P(ang, None, None, box), P(), P(), P(), P()),
        out_specs=P(ang, box),
        check_vma=False,
    )
```

```python
import jax
import jax.numpy as jnp
import numpy as np
from jax import lax
from jax.experimental import pallas as pl
from jax.experimental.pallas import tpu as pltpu
from jax.sharding import Mesh, PartitionSpec as P

AXES = ("y", "z4", "z2", "z1", "c", "zh", "x")
SIZES = (4, 2, 2, 2, 2, 2, 4)
NEAR = ("z2", "z1", "c", "x")
ALL = ("z4", "z2", "z1", "c", "zh", "x")
FLIP_NEAR = 2
FLIP_ALL = 6
K = 576
WIDE = 1280
PACK_VMEM = 60 * 2**20
COLS = 128
PIX = 1024
F32 = jnp.float32
BF16 = jnp.bfloat16
HIGHEST = lax.Precision.HIGHEST
VMEM = pl.BlockSpec(memory_space=pltpu.VMEM)

COS = (
    1.4142134962552286,
    -6.978850948563802,
    5.739460376906949,
    -1.8835579059851506,
    0.31068802752335445,
)
SIN = (
    4.442882919124345,
    -7.308245686509067,
    3.6063542184329913,
    -0.8461116503747359,
    0.10982451642751799,
)

OWN, LOW1, HIGH1, LOW2, HIGH2, ACROSS = range(6)
FREQS = []


def lanes_of(rows, level):
    FREQS.extend((rows, level, d) for d in range(2))
    return len(FREQS) - 2


F0, F1, F2, F3, F4 = (lanes_of(OWN, level) for level in range(5))
UP1 = lanes_of(LOW1, 0), lanes_of(HIGH1, 0)
UP2 = lanes_of(LOW2, 1), lanes_of(HIGH2, 1)
A3, A4 = (lanes_of(ACROSS, level) for level in (3, 4))

SETS = [
    [(-1, F0, 0, 0)],
    [(-1, F0, 0, 1)],
    [(1, UP1[0], 0, 2), (-1, F1, 1, 0)],
    [(1, UP1[1], 0, 2), (-1, F1, 1, 1)],
    [(1, UP2[0], 1, 2), (-1, F2, 2, 0)],
    [(1, UP2[1], 1, 2), (-1, F2, 2, 1)],
    [(1, F2, 2, 2), (-1, F3, 3, None)],
    [(1, F3, 3, 2), (1, F4, 3, 2)],
    [(1, F2, 2, 2), (-1, A3, 3, None)],
    [(1, A3, 3, 2), (1, A4, 3, 2)],
]
HERE = 8
TERMS = [
    (s, sign, lane + d, level, kind, d)
    for s, terms in enumerate(SETS)
    for sign, lane, level, kind in terms
    for d in range(2)
]


def tables():
    pick = np.zeros((6, 16, 256), np.float32)
    for lane, (rows, level, d) in enumerate(FREQS):
        at = level * 2 + d
        for piece in range(3):
            pick[rows, at, 32 * piece + lane] = 1
        for i, term in enumerate(TERMS):
            if term[2] == lane:
                pick[rows, at, 128 + i] = 1
    centre = np.zeros((2, 24, 128), np.float32)
    mask = np.zeros((8, 128), np.float32)
    for i, (s, sign, lane, level, kind, d) in enumerate(TERMS):
        for half in range(2):
            k = half if kind is None else kind
            centre[half, (level * 3 + k) * 2 + d, i] = sign
        mask[FREQS[lane][0], i] = 1
    return pick, centre, mask


PICK, CENTRE, MASK = tables()


def moved(q, rows):
    return {OWN: q, LOW1: q & ~2, HIGH1: q | 2, LOW2: q & ~4, HIGH2: q | 4}[rows]


def prepare_kernel(nodes_ref, cen_ref, centre_ref, mask_ref, pick_ref, out_ref, wide_ref):
    base = lax.axis_index("y") * 16
    half = lax.axis_index("z4")
    turn = 0.5 / np.pi

    def pieces(rest):
        for piece in range(3):
            part = rest.astype(BF16)
            yield piece, part
            rest = rest - part.astype(F32)

    wide_ref[...] = jnp.zeros_like(wide_ref)
    for s, sign, lane, level, kind, d in TERMS:

        def row(kind):
            i = (level * 3 + kind) * 2 + d
            return nodes_ref[i : i + 1, :]

        value = jnp.where(half == 0, row(0), row(1)) if kind is None else row(kind)
        wide_ref[s, lane : lane + 1, :] = value * (sign * turn)
    for s in range(len(SETS)):
        for piece, part in pieces(wide_ref[s]):
            out_ref[s, 32 * piece : 32 * piece + 32, :] = part

    picked = lax.dot_general(
        cen_ref[...] * turn,
        centre_ref[half],
        (((0,), (0,)), ((), ())),
        precision=HIGHEST,
        preferred_element_type=F32,
    )
    q = lax.broadcasted_iota(jnp.int32, (32, 64), 0) & 7
    lane = lax.broadcasted_iota(jnp.int32, (32, 64), 1)
    own = base + half * 8
    across = base + 8 - half * 8
    boxes = [own + q, own + (q & ~2), own + (q | 2), own + (q & ~4), own + (q | 4), across + q]
    total = jnp.zeros((32, 128), F32)
    for v, box in enumerate(boxes):
        hot = jnp.where(lane == box, 1.0, 0.0).astype(F32)
        mine = jnp.dot(hot, picked, precision=HIGHEST, preferred_element_type=F32)
        total = total + mine * mask_ref[v : v + 1, :]
    for piece, part in pieces(total):
        out_ref[10, 32 * piece : 32 * piece + 32, :128] = part
    out_ref[11, :, :256] = pick_ref[...]


def prepare(nodes, cen):
    return pl.pallas_call(
        prepare_kernel,
        out_shape=jax.ShapeDtypeStruct((12, 96, K), BF16),
        in_specs=[VMEM] * 5,
        out_specs=VMEM,
        scratch_shapes=[pltpu.VMEM((10, 32, K), F32)],
        compiler_params=pltpu.CompilerParams(vmem_limit_bytes=6 * 2**20),
        cost_estimate=pl.CostEstimate(flops=10**7, bytes_accessed=5 * 2**20, transcendentals=0),
        name="prepare",
    )(nodes, cen, jnp.asarray(CENTRE), jnp.asarray(MASK), jnp.asarray(PICK.reshape(96, 256), BF16))


def pack_kernel(coeffs_hbm, freqs_hbm, out_ref, coeffs_ref, freqs_ref, sems):
    freqs_copy = pltpu.make_async_copy(freqs_hbm, freqs_ref, sems.at[0])
    coeffs_copy = pltpu.make_async_copy(coeffs_hbm, coeffs_ref, sems.at[1])
    freqs_copy.start()
    coeffs_copy.start()

    def spread(rows):
        i = lax.broadcasted_iota(jnp.int32, (rows, rows), 0)
        j = lax.broadcasted_iota(jnp.int32, (rows, rows), 1)
        half = rows // 2
        return jnp.where(i == 2 * (j % half) + j // half, 1.0, 0.0).astype(BF16)

    def turned(x, y):
        z = lax.dot_general(x, y, (((0,), (0,)), ((), ())), preferred_element_type=F32)
        return z.reshape(32, 4, z.shape[1]).astype(BF16)

    whole, tail = spread(256), spread(128)
    freqs_copy.wait()
    i = lax.broadcasted_iota(jnp.int32, (10, 128), 0)
    j = lax.broadcasted_iota(jnp.int32, (10, 128), 1)
    freqs = freqs_ref[...].astype(F32).reshape(10, COLS).astype(BF16)
    out_ref[:, :, 1152:] = turned(freqs, jnp.where(i == j, 1.0, 0.0).astype(BF16))
    coeffs_copy.wait()
    for m in range(4):
        z = turned(coeffs_ref[m * 256 : m * 256 + 256, :], whole)
        out_ref[:, :, m * 128 : m * 128 + 128] = z[:, :, :128]
        out_ref[:, :, 512 + m * 128 : 512 + m * 128 + 128] = z[:, :, 128:]
    out_ref[:, :, 1024:1152] = turned(coeffs_ref[1024:1152, :], tail)


def pack(coeffs, freqs):
    return pl.pallas_call(
        pack_kernel,
        out_shape=jax.ShapeDtypeStruct((32, 4, WIDE), BF16),
        in_specs=[pl.BlockSpec(memory_space=pl.ANY)] * 2,
        out_specs=VMEM,
        scratch_shapes=[
            pltpu.VMEM((2 * K, COLS), BF16),
            pltpu.VMEM((5, 2, COLS), BF16),
            pltpu.SemaphoreType.DMA((2,)),
        ],
        compiler_params=pltpu.CompilerParams(vmem_limit_bytes=PACK_VMEM),
        cost_estimate=pl.CostEstimate(flops=10**7, bytes_accessed=2**20, transcendentals=0),
        name="pack",
    )(coeffs, freqs)


def horner(coefficients, u):
    total = u * coefficients[-1] + coefficients[-2]
    for value in coefficients[-3::-1]:
        total = total * u + value
    return total


def cos_sin(turns):
    r = turns - jnp.floor(turns + 0.5)
    u = r * r
    sine = r * horner(SIN, u)
    return 1.0 - sine * sine, sine * horner(COS, u)


def dot(a, b):
    return lax.dot_general(a, b, (((1,), (1,)), ((), ())), preferred_element_type=F32)


def block(q):
    return slice(q * 16, q * 16 + 16)


def picked(table_ref, rows, freq):
    pick = table_ref[11, 16 * rows : 16 * rows + 16, :256]
    return jnp.dot(freq, pick, preferred_element_type=F32)


def phases(placed, table_ref, sets, t_ref):
    lanes = placed[:, :96].astype(BF16)
    i = lax.broadcasted_iota(jnp.int32, (128, 128), 0)
    j = lax.broadcasted_iota(jnp.int32, (128, 128), 1)
    first = jnp.where(i < 4, i // 2, (i - 4) // 4 + 2)
    gather = jnp.where((first == j) & (i < len(TERMS)), 1.0, 0.0).astype(F32)
    high, mid, low = (table_ref[10, 32 * p : 32 * p + 32, :128].astype(F32) for p in range(3))
    centre = high + mid + low
    centre = jnp.concatenate(
        [jnp.broadcast_to(centre[q : q + 1], (16, 128)) for q in range(8)], axis=0
    )
    const = jnp.dot(placed[:, 128:] * centre, gather, precision=HIGHEST, preferred_element_type=F32)
    for i, s in enumerate(sets):
        t_ref[i] = jnp.dot(lanes, table_ref[s], preferred_element_type=F32) + const[:, s : s + 1]


def rotated(turns, re, im):
    c, s = cos_sin(turns)
    return c * re - s * im, s * re + c * im


def contribution(state_ref, turns_ref, first, mine, w_ref, s_ref):
    for q in range(8):
        here = block(q)
        re, im = rotated(turns_ref[first, here, :], state_ref[here, :], state_ref[block(q + 8), :])
        w_ref[here, :] = re.astype(BF16)
        w_ref[block(q + 8), :] = im.astype(BF16)
    s_ref[...] = dot(w_ref[...], mine)
    for q in range(8):
        here = block(q)
        c, s = cos_sin(turns_ref[first + 1, here, :])
        v = c * s_ref[here, :] - s * s_ref[block(q + 8), :]
        w_ref[here, :] = v.astype(BF16)
    a = lax.broadcasted_iota(jnp.int32, (32, COLS), 0)
    b = lax.broadcasted_iota(jnp.int32, (32, COLS), 1)
    angles = jnp.where((a // 4 == b // 16) & (a % 4 == b % 4), 1.0, 0.0).astype(BF16)
    return jnp.dot(angles, w_ref[:COLS, :], preferred_element_type=F32).astype(BF16)


def fields(field_ref, q):
    x = field_ref[4 * q : 4 * q + 4].astype(F32).reshape(16, WIDE)
    re = jnp.concatenate([x[:, :512], x[:, 1024:1088]], axis=1)
    im = jnp.concatenate([x[:, 512:1024], x[:, 1088:1152]], axis=1)
    return re, im


def lanes_16(freq_ref):
    return freq_ref[...].astype(F32).reshape(COLS, 128)[:, :16].astype(BF16)


def own_kernel(
    field_ref, freq_ref, table_ref, interp_ref, v_ref, s_ref, low_ref, high_ref, last_ref, t_ref
):
    freq = lanes_16(freq_ref)
    placed = jnp.zeros((COLS, 256), F32)
    for rows in range(ACROSS):
        source = jnp.concatenate([freq[block(moved(q, rows))] for q in range(8)], axis=0)
        placed = placed + picked(table_ref, rows, source)
    phases(placed, table_ref, range(HERE), t_ref)

    for level in range(3):
        for q in range(8):
            here = block(q)
            for kind, w_ref in enumerate((low_ref, high_ref)):
                src = (q & ~(1 << level)) | (kind << level)
                if level == 0:
                    re, im = fields(field_ref, src)
                else:
                    re = s_ref[block(src), :]
                    im = s_ref[block(src + 8), :]
                re, im = rotated(t_ref[2 * level + kind, here, :], re, im)
                w_ref[here, :] = re.astype(BF16)
                w_ref[block(q + 8), :] = im.astype(BF16)
        s_ref[...] = dot(low_ref[...], interp_ref[0]) + dot(high_ref[...], interp_ref[1])
    mine = interp_ref[lax.axis_index("z4")]
    v_ref[...] = contribution(s_ref, t_ref, 6, mine, low_ref, last_ref)


def across_kernel(
    freq_ref,
    freq_across_ref,
    v_ref,
    s_ref,
    table_ref,
    interp_ref,
    eval_ref,
    out_ref,
    w_ref,
    last_ref,
    t_ref,
):
    half = lax.axis_index("z4")
    placed = picked(table_ref, OWN, lanes_16(freq_ref))
    placed = placed + picked(table_ref, ACROSS, lanes_16(freq_across_ref))
    phases(placed, table_ref, (HERE, HERE + 1), t_ref)
    v = contribution(s_ref, t_ref, 0, interp_ref[half], w_ref, last_ref)
    for where, value in ((half, v_ref[...]), (1 - half, v)):
        part = jnp.dot(value, eval_ref[...], preferred_element_type=F32).astype(BF16)
        for p in range(8):
            member = p ^ FLIP_ALL
            out_ref[where, :, p * 128 : p * 128 + 128] = part[:, member * 128 : member * 128 + 128]


def own_levels(field, freq, table, interp):
    return pl.pallas_call(
        own_kernel,
        out_shape=[
            jax.ShapeDtypeStruct((32, K), BF16),
            jax.ShapeDtypeStruct((2 * COLS, K), F32),
        ],
        in_specs=[VMEM] * 4,
        out_specs=[VMEM] * 2,
        scratch_shapes=[
            pltpu.VMEM((2 * COLS, K), BF16),
            pltpu.VMEM((2 * COLS, K), BF16),
            pltpu.VMEM((2 * COLS, K), F32),
            pltpu.VMEM((HERE, COLS, K), F32),
        ],
        compiler_params=pltpu.CompilerParams(vmem_limit_bytes=8 * 2**20),
        cost_estimate=pl.CostEstimate(
            flops=8 * 2 * K * K * 256, bytes_accessed=10 * 2**20, transcendentals=0
        ),
        name="own_levels",
    )(field, freq, table, interp)


def across_level(freq, freq_across, v, state, table, interp, evaluate):
    return pl.pallas_call(
        across_kernel,
        out_shape=jax.ShapeDtypeStruct((2, 32, PIX), BF16),
        in_specs=[VMEM] * 7,
        out_specs=VMEM,
        scratch_shapes=[
            pltpu.VMEM((2 * COLS, K), BF16),
            pltpu.VMEM((2 * COLS, K), F32),
            pltpu.VMEM((2, COLS, K), F32),
        ],
        compiler_params=pltpu.CompilerParams(vmem_limit_bytes=6 * 2**20),
        cost_estimate=pl.CostEstimate(
            flops=2 * 2 * K * K * 256, bytes_accessed=5 * 2**20, transcendentals=0
        ),
        name="across_level",
    )(freq, freq_across, v, state, table, interp, evaluate)


def exchange(block, axes, flip):
    groups = [[i ^ flip for i in range(block.shape[0])]]
    return lax.all_to_all(
        block, axes, split_axis=0, concat_axis=0, tiled=True, axis_index_groups=groups
    )


def body(coeffs, freqs, nodes, centres, interp, evaluate):
    field = exchange(pack(coeffs.reshape(2 * K, COLS), freqs[0]), NEAR, FLIP_NEAR)
    freq = field[:, :, WIDE - 128 :]
    freq_across = lax.ppermute(freq, "z4", [(0, 1), (1, 0)])
    table = prepare(nodes.reshape(24, K), centres.reshape(24, 64))
    v, state = own_levels(field, freq, table, interp)
    part = across_level(freq, freq_across, v, state, table, interp, evaluate.T)
    part = part.reshape(16, 4, 8, 128).transpose(0, 2, 1, 3).reshape(128, 4, 128)
    part = exchange(part, ALL, FLIP_ALL)
    total = jnp.sum(part.reshape(2, 8, 2, 4, 4, 128).astype(F32), axis=(0, 2))
    return total.reshape(COLS, 128).T


def solution(mesh):
    fine = Mesh(mesh.devices.reshape(SIZES), AXES)
    box, ang = ("y", "z4", "z2", "z1", "c"), ("zh", "x")
    return jax.shard_map(
        body,
        mesh=fine,
        in_specs=(P(ang, None, None, box), P(ang, None, None, box), P(), P(), P(), P()),
        out_specs=P(ang, box),
        check_vma=False,
    )
```

```python
import jax
import jax.numpy as jnp
import numpy as np
from jax import lax
from jax.experimental import pallas as pl
from jax.experimental.pallas import tpu as pltpu
from jax.sharding import Mesh, PartitionSpec as P

AXES = ("y", "z4", "z2", "z1", "c", "zh", "x")
SIZES = (4, 2, 2, 2, 2, 2, 4)
NEAR = ("z2", "z1", "c", "x")
ALL = ("z4", "z2", "z1", "c", "zh", "x")
FLIP_NEAR = 10
FLIP_ALL = 6
FLIP_Q = FLIP_NEAR >> 2
FLIP_BACK = FLIP_ALL >> 3 & 7
FLIP_CHUNK = FLIP_NEAR ^ (FLIP_BACK << 2 | FLIP_ALL & 3)
K = 576
WIDE = 1280
PACK_VMEM = 60 * 2**20
COLS = 128
PIX = 1024
F32 = jnp.float32
BF16 = jnp.bfloat16
HIGHEST = lax.Precision.HIGHEST
VMEM = pl.BlockSpec(memory_space=pltpu.VMEM)

COS = (
    1.4142134962552286,
    -6.978850948563802,
    5.739460376906949,
    -1.8835579059851506,
    0.31068802752335445,
)
SIN = (
    4.442882919124345,
    -7.308245686509067,
    3.6063542184329913,
    -0.8461116503747359,
    0.10982451642751799,
)

OWN, LOW1, HIGH1, LOW2, HIGH2, ACROSS = range(6)
FREQS = []


def lanes_of(rows, level):
    FREQS.extend((rows, level, d) for d in range(2))
    return len(FREQS) - 2


F0, F1, F2, F3, F4 = (lanes_of(OWN, level) for level in range(5))
UP1 = lanes_of(LOW1, 0), lanes_of(HIGH1, 0)
UP2 = lanes_of(LOW2, 1), lanes_of(HIGH2, 1)
A3, A4 = (lanes_of(ACROSS, level) for level in (3, 4))

SETS = [
    [(-1, F0, 0, 0)],
    [(-1, F0, 0, 1)],
    [(1, UP1[0], 0, 2), (-1, F1, 1, 0)],
    [(1, UP1[1], 0, 2), (-1, F1, 1, 1)],
    [(1, UP2[0], 1, 2), (-1, F2, 2, 0)],
    [(1, UP2[1], 1, 2), (-1, F2, 2, 1)],
    [(1, F2, 2, 2), (-1, F3, 3, None)],
    [(1, F3, 3, 2), (1, F4, 3, 2)],
    [(1, F2, 2, 2), (-1, A3, 3, None)],
    [(1, A3, 3, 2), (1, A4, 3, 2)],
]
HERE = 8
TERMS = [
    (s, sign, lane + d, level, kind, d)
    for s, terms in enumerate(SETS)
    for sign, lane, level, kind in terms
    for d in range(2)
]


def tables():
    pick = np.zeros((6, 16, 256), np.float32)
    for lane, (rows, level, d) in enumerate(FREQS):
        at = level * 2 + d
        for piece in range(3):
            pick[rows, at, 32 * piece + lane] = 1
        for i, term in enumerate(TERMS):
            if term[2] == lane:
                pick[rows, at, 128 + i] = 1
    centre = np.zeros((2, 24, 128), np.float32)
    mask = np.zeros((8, 128), np.float32)
    for i, (s, sign, lane, level, kind, d) in enumerate(TERMS):
        for half in range(2):
            k = half if kind is None else kind
            centre[half, (level * 3 + k) * 2 + d, i] = sign
        mask[FREQS[lane][0], i] = 1
    return pick, centre, mask


PICK, CENTRE, MASK = tables()


def moved(q, rows):
    box = q ^ FLIP_Q
    box = {OWN: box, LOW1: box & ~2, HIGH1: box | 2, LOW2: box & ~4, HIGH2: box | 4}[rows]
    return box ^ FLIP_Q


def child(q, level, kind):
    box = q ^ FLIP_Q
    return ((box & ~(1 << level)) | (kind << level)) ^ FLIP_Q


def prepare_kernel(nodes_ref, cen_ref, centre_ref, mask_ref, pick_ref, out_ref, wide_ref):
    base = lax.axis_index("y") * 16
    half = lax.axis_index("z4")
    turn = 0.5 / np.pi

    def pieces(rest):
        for piece in range(3):
            part = rest.astype(BF16)
            yield piece, part
            rest = rest - part.astype(F32)

    wide_ref[...] = jnp.zeros_like(wide_ref)
    for s, sign, lane, level, kind, d in TERMS:

        def row(kind):
            i = (level * 3 + kind) * 2 + d
            return nodes_ref[i : i + 1, :]

        value = jnp.where(half == 0, row(0), row(1)) if kind is None else row(kind)
        wide_ref[s, lane : lane + 1, :] = value * (sign * turn)
    for s in range(len(SETS)):
        for piece, part in pieces(wide_ref[s]):
            out_ref[s, 32 * piece : 32 * piece + 32, :] = part

    picked = lax.dot_general(
        cen_ref[...] * turn,
        centre_ref[half],
        (((0,), (0,)), ((), ())),
        precision=HIGHEST,
        preferred_element_type=F32,
    )
    q = lax.broadcasted_iota(jnp.int32, (32, 64), 0) & 7 ^ FLIP_Q
    lane = lax.broadcasted_iota(jnp.int32, (32, 64), 1)
    own = base + half * 8
    across = base + 8 - half * 8
    boxes = [own + q, own + (q & ~2), own + (q | 2), own + (q & ~4), own + (q | 4), across + q]
    total = jnp.zeros((32, 128), F32)
    for v, box in enumerate(boxes):
        hot = jnp.where(lane == box, 1.0, 0.0).astype(F32)
        mine = jnp.dot(hot, picked, precision=HIGHEST, preferred_element_type=F32)
        total = total + mine * mask_ref[v : v + 1, :]
    for piece, part in pieces(total):
        out_ref[10, 32 * piece : 32 * piece + 32, :128] = part
    out_ref[11, :, :256] = pick_ref[...]


def prepare(nodes, cen):
    return pl.pallas_call(
        prepare_kernel,
        out_shape=jax.ShapeDtypeStruct((12, 96, K), BF16),
        in_specs=[VMEM] * 5,
        out_specs=VMEM,
        scratch_shapes=[pltpu.VMEM((10, 32, K), F32)],
        compiler_params=pltpu.CompilerParams(vmem_limit_bytes=6 * 2**20),
        cost_estimate=pl.CostEstimate(flops=10**7, bytes_accessed=5 * 2**20, transcendentals=0),
        name="prepare",
    )(nodes, cen, jnp.asarray(CENTRE), jnp.asarray(MASK), jnp.asarray(PICK.reshape(96, 256), BF16))


def pack_kernel(coeffs_hbm, freqs_hbm, out_ref, coeffs_ref, freqs_ref, sems):
    freqs_copy = pltpu.make_async_copy(freqs_hbm, freqs_ref, sems.at[0])
    coeffs_copy = pltpu.make_async_copy(coeffs_hbm, coeffs_ref, sems.at[1])
    freqs_copy.start()
    coeffs_copy.start()

    def spread(rows):
        i = lax.broadcasted_iota(jnp.int32, (rows, rows), 0)
        j = lax.broadcasted_iota(jnp.int32, (rows, rows), 1)
        half = rows // 2
        return jnp.where(i == 2 * (j % half) + j // half, 1.0, 0.0).astype(BF16)

    def turned(x, y):
        z = lax.dot_general(x, y, (((0,), (0,)), ((), ())), preferred_element_type=F32)
        z = z.reshape(32, 4, z.shape[1])
        if FLIP_CHUNK:
            z = jnp.concatenate([z[i ^ FLIP_CHUNK : (i ^ FLIP_CHUNK) + 1] for i in range(32)], axis=0)
        return z.astype(BF16)

    whole, tail = spread(256), spread(128)
    freqs_copy.wait()
    i = lax.broadcasted_iota(jnp.int32, (10, 128), 0)
    j = lax.broadcasted_iota(jnp.int32, (10, 128), 1)
    freqs = freqs_ref[...].astype(F32).reshape(10, COLS).astype(BF16)
    out_ref[:, :, 1152:] = turned(freqs, jnp.where(i == j, 1.0, 0.0).astype(BF16))
    coeffs_copy.wait()
    for m in range(4):
        z = turned(coeffs_ref[m * 256 : m * 256 + 256, :], whole)
        out_ref[:, :, m * 128 : m * 128 + 128] = z[:, :, :128]
        out_ref[:, :, 512 + m * 128 : 512 + m * 128 + 128] = z[:, :, 128:]
    out_ref[:, :, 1024:1152] = turned(coeffs_ref[1024:1152, :], tail)


def pack(coeffs, freqs):
    return pl.pallas_call(
        pack_kernel,
        out_shape=jax.ShapeDtypeStruct((32, 4, WIDE), BF16),
        in_specs=[pl.BlockSpec(memory_space=pl.ANY)] * 2,
        out_specs=VMEM,
        scratch_shapes=[
            pltpu.VMEM((2 * K, COLS), BF16),
            pltpu.VMEM((5, 2, COLS), BF16),
            pltpu.SemaphoreType.DMA((2,)),
        ],
        compiler_params=pltpu.CompilerParams(vmem_limit_bytes=PACK_VMEM),
        cost_estimate=pl.CostEstimate(flops=10**7, bytes_accessed=2**20, transcendentals=0),
        name="pack",
    )(coeffs, freqs)


def horner(coefficients, u):
    total = u * coefficients[-1] + coefficients[-2]
    for value in coefficients[-3::-1]:
        total = total * u + value
    return total


def cos_sin(turns):
    r = turns - jnp.floor(turns + 0.5)
    u = r * r
    sine = r * horner(SIN, u)
    return 1.0 - sine * sine, sine * horner(COS, u)


def dot(a, b):
    return lax.dot_general(a, b, (((1,), (1,)), ((), ())), preferred_element_type=F32)


def block(q):
    return slice(q * 16, q * 16 + 16)


def picked(table_ref, rows, freq):
    pick = table_ref[11, 16 * rows : 16 * rows + 16, :256]
    return jnp.dot(freq, pick, preferred_element_type=F32)


def phases(placed, table_ref, sets, t_ref):
    lanes = placed[:, :96].astype(BF16)
    i = lax.broadcasted_iota(jnp.int32, (128, 128), 0)
    j = lax.broadcasted_iota(jnp.int32, (128, 128), 1)
    first = jnp.where(i < 4, i // 2, (i - 4) // 4 + 2)
    gather = jnp.where((first == j) & (i < len(TERMS)), 1.0, 0.0).astype(F32)
    high, mid, low = (table_ref[10, 32 * p : 32 * p + 32, :128].astype(F32) for p in range(3))
    centre = high + mid + low
    centre = jnp.concatenate(
        [jnp.broadcast_to(centre[q : q + 1], (16, 128)) for q in range(8)], axis=0
    )
    const = jnp.dot(placed[:, 128:] * centre, gather, precision=HIGHEST, preferred_element_type=F32)
    for i, s in enumerate(sets):
        t_ref[i] = jnp.dot(lanes, table_ref[s], preferred_element_type=F32) + const[:, s : s + 1]


def rotated(turns, re, im):
    c, s = cos_sin(turns)
    return c * re - s * im, s * re + c * im


def contribution(state_ref, turns_ref, first, mine, w_ref, s_ref):
    for q in range(8):
        here = block(q)
        re, im = rotated(turns_ref[first, here, :], state_ref[here, :], state_ref[block(q + 8), :])
        w_ref[here, :] = re.astype(BF16)
        w_ref[block(q + 8), :] = im.astype(BF16)
    s_ref[...] = dot(w_ref[...], mine)
    for q in range(8):
        here = block(q)
        c, s = cos_sin(turns_ref[first + 1, here, :])
        v = c * s_ref[here, :] - s * s_ref[block(q + 8), :]
        w_ref[here, :] = v.astype(BF16)
    a = lax.broadcasted_iota(jnp.int32, (32, COLS), 0)
    b = lax.broadcasted_iota(jnp.int32, (32, COLS), 1)
    box = b // 16 ^ FLIP_Q ^ FLIP_BACK
    angles = jnp.where((a // 4 == box) & (a % 4 == b % 4), 1.0, 0.0).astype(BF16)
    return jnp.dot(angles, w_ref[:COLS, :], preferred_element_type=F32).astype(BF16)


def fields(field_ref, q):
    x = field_ref[4 * q : 4 * q + 4].astype(F32).reshape(16, WIDE)
    re = jnp.concatenate([x[:, :512], x[:, 1024:1088]], axis=1)
    im = jnp.concatenate([x[:, 512:1024], x[:, 1088:1152]], axis=1)
    return re, im


def lanes_16(freq_ref):
    return freq_ref[...].astype(F32).reshape(COLS, 128)[:, :16].astype(BF16)


def own_kernel(
    field_ref, freq_ref, table_ref, interp_ref, v_ref, s_ref, low_ref, high_ref, last_ref, t_ref
):
    freq = lanes_16(freq_ref)
    placed = jnp.zeros((COLS, 256), F32)
    for rows in range(ACROSS):
        source = jnp.concatenate([freq[block(moved(q, rows))] for q in range(8)], axis=0)
        placed = placed + picked(table_ref, rows, source)
    phases(placed, table_ref, range(HERE), t_ref)

    for level in range(3):
        for q in range(8):
            here = block(q)
            for kind, w_ref in enumerate((low_ref, high_ref)):
                src = child(q, level, kind)
                if level == 0:
                    re, im = fields(field_ref, src)
                else:
                    re = s_ref[block(src), :]
                    im = s_ref[block(src + 8), :]
                re, im = rotated(t_ref[2 * level + kind, here, :], re, im)
                w_ref[here, :] = re.astype(BF16)
                w_ref[block(q + 8), :] = im.astype(BF16)
        s_ref[...] = dot(low_ref[...], interp_ref[0]) + dot(high_ref[...], interp_ref[1])
    mine = interp_ref[lax.axis_index("z4")]
    v_ref[...] = contribution(s_ref, t_ref, 6, mine, low_ref, last_ref)


def across_kernel(
    freq_ref,
    freq_across_ref,
    v_ref,
    s_ref,
    table_ref,
    interp_ref,
    eval_ref,
    out_ref,
    w_ref,
    last_ref,
    t_ref,
):
    half = lax.axis_index("z4")
    place = half ^ (FLIP_ALL >> 6)
    placed = picked(table_ref, OWN, lanes_16(freq_ref))
    placed = placed + picked(table_ref, ACROSS, lanes_16(freq_across_ref))
    phases(placed, table_ref, (HERE, HERE + 1), t_ref)
    v = contribution(s_ref, t_ref, 0, interp_ref[half], w_ref, last_ref)
    for where, value in ((place, v_ref[...]), (1 - place, v)):
        part = jnp.dot(value, eval_ref[...], preferred_element_type=F32)
        part = part.reshape(8, 4, PIX).astype(BF16)
        for p in range(8):
            member = p ^ FLIP_ALL & 7
            out_ref[where, :, p] = part[:, :, member * 128 : member * 128 + 128]


def own_levels(field, freq, table, interp):
    return pl.pallas_call(
        own_kernel,
        out_shape=[
            jax.ShapeDtypeStruct((32, K), BF16),
            jax.ShapeDtypeStruct((2 * COLS, K), F32),
        ],
        in_specs=[VMEM] * 4,
        out_specs=[VMEM] * 2,
        scratch_shapes=[
            pltpu.VMEM((2 * COLS, K), BF16),
            pltpu.VMEM((2 * COLS, K), BF16),
            pltpu.VMEM((2 * COLS, K), F32),
            pltpu.VMEM((HERE, COLS, K), F32),
        ],
        compiler_params=pltpu.CompilerParams(vmem_limit_bytes=8 * 2**20),
        cost_estimate=pl.CostEstimate(
            flops=8 * 2 * K * K * 256, bytes_accessed=10 * 2**20, transcendentals=0
        ),
        name="own_levels",
    )(field, freq, table, interp)


def across_level(freq, freq_across, v, state, table, interp, evaluate):
    return pl.pallas_call(
        across_kernel,
        out_shape=jax.ShapeDtypeStruct((2, 8, 8, 4, 128), BF16),
        in_specs=[VMEM] * 7,
        out_specs=VMEM,
        scratch_shapes=[
            pltpu.VMEM((2 * COLS, K), BF16),
            pltpu.VMEM((2 * COLS, K), F32),
            pltpu.VMEM((2, COLS, K), F32),
        ],
        compiler_params=pltpu.CompilerParams(vmem_limit_bytes=6 * 2**20),
        cost_estimate=pl.CostEstimate(
            flops=2 * 2 * K * K * 256, bytes_accessed=5 * 2**20, transcendentals=0
        ),
        name="across_level",
    )(freq, freq_across, v, state, table, interp, evaluate)


def exchange(block, axes, flip):
    groups = [[i ^ flip for i in range(block.shape[0])]]
    return lax.all_to_all(
        block, axes, split_axis=0, concat_axis=0, tiled=True, axis_index_groups=groups
    )


def body(coeffs, freqs, nodes, centres, interp, evaluate):
    field = exchange(pack(coeffs.reshape(2 * K, COLS), freqs[0]), NEAR, FLIP_NEAR)
    freq = field[:, :, WIDE - 128 :]
    freq_across = lax.ppermute(freq, "z4", [(0, 1), (1, 0)])
    table = prepare(nodes.reshape(24, K), centres.reshape(24, 64))
    v, state = own_levels(field, freq, table, interp)
    part = across_level(freq, freq_across, v, state, table, interp, evaluate.T)
    part = part.reshape(128, 4, 128)
    part = exchange(part, ALL, FLIP_ALL)
    total = jnp.sum(part.reshape(2, 8, 2, 4, 4, 128).astype(F32), axis=(0, 2))
    return total.reshape(COLS, 128).T


def solution(mesh):
    fine = Mesh(mesh.devices.reshape(SIZES), AXES)
    box, ang = ("y", "z4", "z2", "z1", "c"), ("zh", "x")
    return jax.shard_map(
        body,
        mesh=fine,
        in_specs=(P(ang, None, None, box), P(ang, None, None, box), P(), P(), P(), P()),
        out_specs=P(ang, box),
        check_vma=False,
    )
```

```python
import jax
import jax.numpy as jnp
import numpy as np
from jax import lax
from jax.experimental import pallas as pl
from jax.experimental.pallas import tpu as pltpu
from jax.sharding import Mesh, PartitionSpec as P

AXES = ("y", "z4", "z2", "z1", "c", "zh", "x")
SIZES = (4, 2, 2, 2, 2, 2, 4)
NEAR = ("z2", "z1", "c", "x")
ALL = ("z4", "z2", "z1", "c", "zh", "x")
FLIP_NEAR = 10
FLIP_ALL = 6
FLIP_Q = FLIP_NEAR >> 2
FLIP_BACK = FLIP_ALL >> 3 & 7
FLIP_CHUNK = FLIP_NEAR ^ (FLIP_BACK << 2 | FLIP_ALL & 3)
SPOTS = 16
K = 576
WIDE = 1280
PACK_VMEM = 60 * 2**20
COLS = 128
PIX = 1024
F32 = jnp.float32
BF16 = jnp.bfloat16
HIGHEST = lax.Precision.HIGHEST
VMEM = pl.BlockSpec(memory_space=pltpu.VMEM)

COS = (
    1.4142134962552286,
    -6.978850948563802,
    5.739460376906949,
    -1.8835579059851506,
    0.31068802752335445,
)
SIN = (
    4.442882919124345,
    -7.308245686509067,
    3.6063542184329913,
    -0.8461116503747359,
    0.10982451642751799,
)

OWN, LOW1, HIGH1, LOW2, HIGH2, ACROSS = range(6)
FREQS = []


def lanes_of(rows, level):
    FREQS.extend((rows, level, d) for d in range(2))
    return len(FREQS) - 2


F0, F1, F2, F3, F4 = (lanes_of(OWN, level) for level in range(5))
UP1 = lanes_of(LOW1, 0), lanes_of(HIGH1, 0)
UP2 = lanes_of(LOW2, 1), lanes_of(HIGH2, 1)
A3, A4 = (lanes_of(ACROSS, level) for level in (3, 4))

SETS = [
    [(-1, F0, 0, 0)],
    [(-1, F0, 0, 1)],
    [(1, UP1[0], 0, 2), (-1, F1, 1, 0)],
    [(1, UP1[1], 0, 2), (-1, F1, 1, 1)],
    [(1, UP2[0], 1, 2), (-1, F2, 2, 0)],
    [(1, UP2[1], 1, 2), (-1, F2, 2, 1)],
    [(1, F2, 2, 2), (-1, F3, 3, None)],
    [(1, F3, 3, 2), (1, F4, 3, 2)],
    [(1, F2, 2, 2), (-1, A3, 3, None)],
    [(1, A3, 3, 2), (1, A4, 3, 2)],
]
HERE = 8
TERMS = [
    (s, sign, lane + d, level, kind, d)
    for s, terms in enumerate(SETS)
    for sign, lane, level, kind in terms
    for d in range(2)
]


def tables():
    pick = np.zeros((6, 16, 256), np.float32)
    for lane, (rows, level, d) in enumerate(FREQS):
        at = level * 2 + d
        for piece in range(3):
            pick[rows, at, 32 * piece + lane] = 1
        for i, term in enumerate(TERMS):
            if term[2] == lane:
                pick[rows, at, 128 + i] = 1
    spots = np.zeros((96, 256), np.float32)
    for i in range(64):
        spots[i] = pick[ACROSS, 6 + i % 4]
    centre = np.zeros((2, 24, 128), np.float32)
    mask = np.zeros((8, 128), np.float32)
    for i, (s, sign, lane, level, kind, d) in enumerate(TERMS):
        for half in range(2):
            k = half if kind is None else kind
            centre[half, (level * 3 + k) * 2 + d, i] = sign
        mask[FREQS[lane][0], i] = 1
    pick = np.concatenate([pick.reshape(96, 256), spots], axis=1)
    return pick, centre, mask


PICK, CENTRE, MASK = tables()


def moved(q, rows):
    box = q ^ FLIP_Q
    box = {OWN: box, LOW1: box & ~2, HIGH1: box | 2, LOW2: box & ~4, HIGH2: box | 4}[rows]
    return box ^ FLIP_Q


def child(q, level, kind):
    box = q ^ FLIP_Q
    return ((box & ~(1 << level)) | (kind << level)) ^ FLIP_Q


def prepare_kernel(nodes_ref, cen_ref, centre_ref, mask_ref, pick_ref, out_ref, wide_ref):
    base = lax.axis_index("y") * 16
    half = lax.axis_index("z4")
    turn = 0.5 / np.pi

    def pieces(rest):
        for piece in range(3):
            part = rest.astype(BF16)
            yield piece, part
            rest = rest - part.astype(F32)

    wide_ref[...] = jnp.zeros_like(wide_ref)
    for s, sign, lane, level, kind, d in TERMS:

        def row(kind):
            i = (level * 3 + kind) * 2 + d
            return nodes_ref[i : i + 1, :]

        value = jnp.where(half == 0, row(0), row(1)) if kind is None else row(kind)
        wide_ref[s, lane : lane + 1, :] = value * (sign * turn)
    for s in range(len(SETS)):
        for piece, part in pieces(wide_ref[s]):
            out_ref[s, 32 * piece : 32 * piece + 32, :] = part

    picked = lax.dot_general(
        cen_ref[...] * turn,
        centre_ref[half],
        (((0,), (0,)), ((), ())),
        precision=HIGHEST,
        preferred_element_type=F32,
    )
    q = lax.broadcasted_iota(jnp.int32, (32, 64), 0) & 7 ^ FLIP_Q
    lane = lax.broadcasted_iota(jnp.int32, (32, 64), 1)
    own = base + half * 8
    across = base + 8 - half * 8
    boxes = [own + q, own + (q & ~2), own + (q | 2), own + (q & ~4), own + (q | 4), across + q]
    total = jnp.zeros((32, 128), F32)
    for v, box in enumerate(boxes):
        hot = jnp.where(lane == box, 1.0, 0.0).astype(F32)
        mine = jnp.dot(hot, picked, precision=HIGHEST, preferred_element_type=F32)
        total = total + mine * mask_ref[v : v + 1, :]
    for piece, part in pieces(total):
        out_ref[10, 32 * piece : 32 * piece + 32, :128] = part
    out_ref[11, :, :512] = pick_ref[...]


def prepare(nodes, cen):
    return pl.pallas_call(
        prepare_kernel,
        out_shape=jax.ShapeDtypeStruct((12, 96, K), BF16),
        in_specs=[VMEM] * 5,
        out_specs=VMEM,
        scratch_shapes=[pltpu.VMEM((10, 32, K), F32)],
        compiler_params=pltpu.CompilerParams(vmem_limit_bytes=6 * 2**20),
        cost_estimate=pl.CostEstimate(flops=10**7, bytes_accessed=5 * 2**20, transcendentals=0),
        name="prepare",
    )(nodes, cen, jnp.asarray(CENTRE), jnp.asarray(MASK), jnp.asarray(PICK, BF16))


def pack_kernel(coeffs_hbm, freqs_hbm, out_ref, coeffs_ref, freqs_ref, sems):
    freqs_copy = pltpu.make_async_copy(freqs_hbm, freqs_ref, sems.at[0])
    coeffs_copy = pltpu.make_async_copy(coeffs_hbm, coeffs_ref, sems.at[1])
    freqs_copy.start()
    coeffs_copy.start()

    def spread(rows):
        i = lax.broadcasted_iota(jnp.int32, (rows, rows), 0)
        j = lax.broadcasted_iota(jnp.int32, (rows, rows), 1)
        half = rows // 2
        return jnp.where(i == 2 * (j % half) + j // half, 1.0, 0.0).astype(BF16)

    def turned(x, y):
        z = lax.dot_general(x, y, (((0,), (0,)), ((), ())), preferred_element_type=F32)
        z = z.reshape(32, 4, z.shape[1])
        if FLIP_CHUNK:
            z = jnp.concatenate([z[i ^ FLIP_CHUNK : (i ^ FLIP_CHUNK) + 1] for i in range(32)], axis=0)
        return z.astype(BF16)

    whole, tail = spread(256), spread(128)
    freqs_copy.wait()
    i = lax.broadcasted_iota(jnp.int32, (10, 128), 0)
    j = lax.broadcasted_iota(jnp.int32, (10, 128), 1)
    position = lax.axis_index(NEAR) ^ FLIP_NEAR
    spot = SPOTS + 4 * (position & 15)
    hot = (i == j) | ((i > 5) & (j == i - 6 + spot))
    freqs = freqs_ref[...].astype(F32).reshape(10, COLS).astype(BF16)
    out_ref[:, :, 1152:] = turned(freqs, jnp.where(hot, 1.0, 0.0).astype(BF16))
    coeffs_copy.wait()
    for m in range(4):
        z = turned(coeffs_ref[m * 256 : m * 256 + 256, :], whole)
        out_ref[:, :, m * 128 : m * 128 + 128] = z[:, :, :128]
        out_ref[:, :, 512 + m * 128 : 512 + m * 128 + 128] = z[:, :, 128:]
    out_ref[:, :, 1024:1152] = turned(coeffs_ref[1024:1152, :], tail)


def pack(coeffs, freqs):
    return pl.pallas_call(
        pack_kernel,
        out_shape=jax.ShapeDtypeStruct((32, 4, WIDE), BF16),
        in_specs=[pl.BlockSpec(memory_space=pl.ANY)] * 2,
        out_specs=VMEM,
        scratch_shapes=[
            pltpu.VMEM((2 * K, COLS), BF16),
            pltpu.VMEM((5, 2, COLS), BF16),
            pltpu.SemaphoreType.DMA((2,)),
        ],
        compiler_params=pltpu.CompilerParams(vmem_limit_bytes=PACK_VMEM),
        cost_estimate=pl.CostEstimate(flops=10**7, bytes_accessed=2**20, transcendentals=0),
        name="pack",
    )(coeffs, freqs)


def horner(coefficients, u):
    total = u * coefficients[-1] + coefficients[-2]
    for value in coefficients[-3::-1]:
        total = total * u + value
    return total


def cos_sin(turns):
    r = turns - jnp.floor(turns + 0.5)
    u = r * r
    sine = r * horner(SIN, u)
    return 1.0 - sine * sine, sine * horner(COS, u)


def dot(a, b):
    return lax.dot_general(a, b, (((1,), (1,)), ((), ())), preferred_element_type=F32)


def block(q):
    return slice(q * 16, q * 16 + 16)


def pieces(rest):
    for _ in range(3):
        part = rest.astype(BF16)
        yield part
        rest = rest - part.astype(F32)


def picked(table_ref, rows, freq):
    pick = table_ref[11, 16 * rows : 16 * rows + 16, :256]
    return jnp.dot(freq, pick, preferred_element_type=F32)


def phases(placed, table_ref, sets, t_ref):
    lanes = placed[:, :96].astype(BF16)
    i = lax.broadcasted_iota(jnp.int32, (128, 128), 0)
    j = lax.broadcasted_iota(jnp.int32, (128, 128), 1)
    first = jnp.where(i < 4, i // 2, (i - 4) // 4 + 2)
    gather = jnp.where((first == j) & (i < len(TERMS)), 1.0, 0.0).astype(F32)
    high, mid, low = (table_ref[10, 32 * p : 32 * p + 32, :128].astype(F32) for p in range(3))
    centre = high + mid + low
    centre = jnp.concatenate(
        [jnp.broadcast_to(centre[q : q + 1], (16, 128)) for q in range(8)], axis=0
    )
    const = sum(
        jnp.dot(part, gather.astype(BF16), preferred_element_type=F32)
        for part in pieces(placed[:, 128:] * centre)
    )
    for i, s in enumerate(sets):
        t_ref[i] = jnp.dot(lanes, table_ref[s], preferred_element_type=F32) + const[:, s : s + 1]


def rotated(turns, re, im):
    c, s = cos_sin(turns)
    return c * re - s * im, s * re + c * im


def contribution(state_ref, turns_ref, first, mine, w_ref, s_ref):
    for q in range(8):
        here = block(q)
        re, im = rotated(turns_ref[first, here, :], state_ref[here, :], state_ref[block(q + 8), :])
        w_ref[here, :] = re.astype(BF16)
        w_ref[block(q + 8), :] = im.astype(BF16)
    s_ref[...] = dot(w_ref[...], mine)
    for q in range(8):
        here = block(q)
        c, s = cos_sin(turns_ref[first + 1, here, :])
        v = c * s_ref[here, :] - s * s_ref[block(q + 8), :]
        w_ref[here, :] = v.astype(BF16)
    a = lax.broadcasted_iota(jnp.int32, (32, COLS), 0)
    b = lax.broadcasted_iota(jnp.int32, (32, COLS), 1)
    box = b // 16 ^ FLIP_Q ^ FLIP_BACK
    angles = jnp.where((a // 4 == box) & (a % 4 == b % 4), 1.0, 0.0).astype(BF16)
    return jnp.dot(angles, w_ref[:COLS, :], preferred_element_type=F32).astype(BF16)


def fields(field_ref, q):
    x = field_ref[4 * q : 4 * q + 4].astype(F32).reshape(16, WIDE)
    re = jnp.concatenate([x[:, :512], x[:, 1024:1088]], axis=1)
    im = jnp.concatenate([x[:, 512:1024], x[:, 1088:1152]], axis=1)
    return re, im


def lanes_16(freq_ref):
    return freq_ref[...].astype(F32).reshape(COLS, 128)[:, :16].astype(BF16)


def own_kernel(
    field_ref, freq_ref, table_ref, interp_ref, v_ref, s_ref, low_ref, high_ref, last_ref, t_ref
):
    freq = lanes_16(freq_ref)
    placed = jnp.zeros((COLS, 256), F32)
    for rows in range(ACROSS):
        source = jnp.concatenate([freq[block(moved(q, rows))] for q in range(8)], axis=0)
        placed = placed + picked(table_ref, rows, source)
    phases(placed, table_ref, range(HERE), t_ref)

    for level in range(3):
        for q in range(8):
            here = block(q)
            for kind, w_ref in enumerate((low_ref, high_ref)):
                src = child(q, level, kind)
                if level == 0:
                    re, im = fields(field_ref, src)
                else:
                    re = s_ref[block(src), :]
                    im = s_ref[block(src + 8), :]
                re, im = rotated(t_ref[2 * level + kind, here, :], re, im)
                w_ref[here, :] = re.astype(BF16)
                w_ref[block(q + 8), :] = im.astype(BF16)
        s_ref[...] = dot(low_ref[...], interp_ref[0]) + dot(high_ref[...], interp_ref[1])
    mine = interp_ref[lax.axis_index("z4")]
    v_ref[...] = contribution(s_ref, t_ref, 6, mine, low_ref, last_ref)


def across_kernel(
    freq_ref,
    freq_across_ref,
    v_ref,
    s_ref,
    table_ref,
    interp_ref,
    eval_ref,
    out_ref,
    w_ref,
    last_ref,
    t_ref,
):
    half = lax.axis_index("z4")
    place = half ^ (FLIP_ALL >> 6)
    placed = picked(table_ref, OWN, lanes_16(freq_ref))
    across = freq_across_ref[...].astype(F32)[:, None]
    across = jnp.broadcast_to(across, (2, 16, 4, 128)).reshape(COLS, 128)
    across = across[:, SPOTS : SPOTS + 64]
    a = lax.broadcasted_iota(jnp.int32, (COLS, 64), 0)
    b = lax.broadcasted_iota(jnp.int32, (COLS, 64), 1)
    across = jnp.where(a // 4 % 16 == b // 4, across, 0.0).astype(BF16)
    placed = placed + jnp.dot(across, table_ref[11, :64, 256:512], preferred_element_type=F32)
    phases(placed, table_ref, (HERE, HERE + 1), t_ref)
    v = contribution(s_ref, t_ref, 0, interp_ref[half], w_ref, last_ref)
    for where, value in ((place, v_ref[...]), (1 - place, v)):
        part = jnp.dot(value, eval_ref[...], preferred_element_type=F32)
        part = part.reshape(8, 4, PIX).astype(BF16)
        for p in range(8):
            member = p ^ FLIP_ALL & 7
            out_ref[where, :, p] = part[:, :, member * 128 : member * 128 + 128]


def own_levels(field, freq, table, interp):
    return pl.pallas_call(
        own_kernel,
        out_shape=[
            jax.ShapeDtypeStruct((32, K), BF16),
            jax.ShapeDtypeStruct((2 * COLS, K), F32),
        ],
        in_specs=[VMEM] * 4,
        out_specs=[VMEM] * 2,
        scratch_shapes=[
            pltpu.VMEM((2 * COLS, K), BF16),
            pltpu.VMEM((2 * COLS, K), BF16),
            pltpu.VMEM((2 * COLS, K), F32),
            pltpu.VMEM((HERE, COLS, K), F32),
        ],
        compiler_params=pltpu.CompilerParams(vmem_limit_bytes=8 * 2**20),
        cost_estimate=pl.CostEstimate(
            flops=8 * 2 * K * K * 256, bytes_accessed=10 * 2**20, transcendentals=0
        ),
        name="own_levels",
    )(field, freq, table, interp)


def across_level(freq, freq_across, v, state, table, interp, evaluate):
    return pl.pallas_call(
        across_kernel,
        out_shape=jax.ShapeDtypeStruct((2, 8, 8, 4, 128), BF16),
        in_specs=[VMEM] * 7,
        out_specs=VMEM,
        scratch_shapes=[
            pltpu.VMEM((2 * COLS, K), BF16),
            pltpu.VMEM((2 * COLS, K), F32),
            pltpu.VMEM((2, COLS, K), F32),
        ],
        compiler_params=pltpu.CompilerParams(vmem_limit_bytes=6 * 2**20),
        cost_estimate=pl.CostEstimate(
            flops=2 * 2 * K * K * 256, bytes_accessed=5 * 2**20, transcendentals=0
        ),
        name="across_level",
    )(freq, freq_across, v, state, table, interp, evaluate)


def exchange(block, axes, flip):
    groups = [[i ^ flip for i in range(block.shape[0])]]
    return lax.all_to_all(
        block, axes, split_axis=0, concat_axis=0, tiled=True, axis_index_groups=groups
    )


def body(coeffs, freqs, nodes, centres, interp, evaluate):
    field = exchange(pack(coeffs.reshape(2 * K, COLS), freqs[0]), NEAR, FLIP_NEAR)
    freq = field[:, :, WIDE - 128 :]
    spots = jnp.sum(freq.reshape(2, 16, 4, 128).astype(F32), axis=1).astype(BF16)
    freq_across = lax.ppermute(spots, "z4", [(0, 1), (1, 0)])
    table = prepare(nodes.reshape(24, K), centres.reshape(24, 64))
    v, state = own_levels(field, freq, table, interp)
    part = across_level(freq, freq_across, v, state, table, interp, evaluate.T)
    part = part.reshape(128, 4, 128)
    part = exchange(part, ALL, FLIP_ALL)
    total = jnp.sum(part.reshape(2, 8, 2, 4, 4, 128).astype(F32), axis=(0, 2))
    return total.reshape(COLS, 128).T


def solution(mesh):
    fine = Mesh(mesh.devices.reshape(SIZES), AXES)
    box, ang = ("y", "z4", "z2", "z1", "c"), ("zh", "x")
    return jax.shard_map(
        body,
        mesh=fine,
        in_specs=(P(ang, None, None, box), P(ang, None, None, box), P(), P(), P(), P()),
        out_specs=P(ang, box),
        check_vma=False,
    )
```

```python
import jax
import jax.numpy as jnp
import numpy as np
from jax import lax
from jax.experimental import pallas as pl
from jax.experimental.pallas import tpu as pltpu
from jax.sharding import Mesh, PartitionSpec as P

AXES = ("y", "z4", "z2", "z1", "c", "zh", "x")
SIZES = (4, 2, 2, 2, 2, 2, 4)
NEAR = ("z2", "z1", "c", "x")
ALL = ("z4", "z2", "z1", "c", "zh", "x")
FLIP_NEAR = 10
FLIP_ALL = 6
FLIP_Q = FLIP_NEAR >> 2
FLIP_BACK = FLIP_ALL >> 3 & 7
FLIP_CHUNK = FLIP_NEAR ^ (FLIP_BACK << 2 | FLIP_ALL & 3)
SPOTS = 16
K = 576
WIDE = 1280
PACK_VMEM = 60 * 2**20
COLS = 128
PIX = 1024
F32 = jnp.float32
BF16 = jnp.bfloat16
HIGHEST = lax.Precision.HIGHEST
VMEM = pl.BlockSpec(memory_space=pltpu.VMEM)

COS = (
    1.4142134962552286,
    -6.978850948563802,
    5.739460376906949,
    -1.8835579059851506,
    0.31068802752335445,
)
SIN = (
    4.442882919124345,
    -7.308245686509067,
    3.6063542184329913,
    -0.8461116503747359,
    0.10982451642751799,
)

OWN, LOW1, HIGH1, LOW2, HIGH2, ACROSS = range(6)
FREQS = []


def lanes_of(rows, level):
    FREQS.extend((rows, level, d) for d in range(2))
    return len(FREQS) - 2


F0, F1, F2, F3, F4 = (lanes_of(OWN, level) for level in range(5))
UP1 = lanes_of(LOW1, 0), lanes_of(HIGH1, 0)
UP2 = lanes_of(LOW2, 1), lanes_of(HIGH2, 1)
A3, A4 = (lanes_of(ACROSS, level) for level in (3, 4))

SETS = [
    [(-1, F0, 0, 0)],
    [(-1, F0, 0, 1)],
    [(1, UP1[0], 0, 2), (-1, F1, 1, 0)],
    [(1, UP1[1], 0, 2), (-1, F1, 1, 1)],
    [(1, UP2[0], 1, 2), (-1, F2, 2, 0)],
    [(1, UP2[1], 1, 2), (-1, F2, 2, 1)],
    [(1, F2, 2, 2), (-1, F3, 3, None)],
    [(1, F3, 3, 2), (1, F4, 3, 2)],
    [(1, F2, 2, 2), (-1, A3, 3, None)],
    [(1, A3, 3, 2), (1, A4, 3, 2)],
]
HERE = 8
TERMS = [
    (s, sign, lane + d, level, kind, d)
    for s, terms in enumerate(SETS)
    for sign, lane, level, kind in terms
    for d in range(2)
]


def tables():
    pick = np.zeros((6, 16, 256), np.float32)
    for lane, (rows, level, d) in enumerate(FREQS):
        at = level * 2 + d
        for piece in range(3):
            pick[rows, at, 32 * piece + lane] = 1
        for i, term in enumerate(TERMS):
            if term[2] == lane:
                pick[rows, at, 128 + i] = 1
    spots = np.zeros((96, 256), np.float32)
    for i in range(64):
        spots[i] = pick[ACROSS, 6 + i % 4]
    centre = np.zeros((2, 24, 128), np.float32)
    mask = np.zeros((8, 128), np.float32)
    for i, (s, sign, lane, level, kind, d) in enumerate(TERMS):
        for half in range(2):
            k = half if kind is None else kind
            centre[half, (level * 3 + k) * 2 + d, i] = sign
        mask[FREQS[lane][0], i] = 1
    pick = np.concatenate([pick.reshape(96, 256), spots], axis=1)
    return pick, centre, mask


PICK, CENTRE, MASK = tables()


def moved(q, rows):
    box = q ^ FLIP_Q
    box = {OWN: box, LOW1: box & ~2, HIGH1: box | 2, LOW2: box & ~4, HIGH2: box | 4}[rows]
    return box ^ FLIP_Q


def child(q, level, kind):
    box = q ^ FLIP_Q
    return ((box & ~(1 << level)) | (kind << level)) ^ FLIP_Q


def prepare_kernel(nodes_ref, cen_ref, centre_ref, mask_ref, pick_ref, out_ref, wide_ref):
    base = lax.axis_index("y") * 16
    half = lax.axis_index("z4")
    turn = 0.5 / np.pi

    def pieces(rest):
        for piece in range(3):
            part = rest.astype(BF16)
            yield piece, part
            rest = rest - part.astype(F32)

    wide_ref[...] = jnp.zeros_like(wide_ref)
    for s, sign, lane, level, kind, d in TERMS:

        def row(kind):
            i = (level * 3 + kind) * 2 + d
            return nodes_ref[i : i + 1, :]

        value = jnp.where(half == 0, row(0), row(1)) if kind is None else row(kind)
        wide_ref[s, lane : lane + 1, :] = value * (sign * turn)
    for s in range(len(SETS)):
        for piece, part in pieces(wide_ref[s]):
            out_ref[s, 32 * piece : 32 * piece + 32, :] = part

    picked = lax.dot_general(
        cen_ref[...] * turn,
        centre_ref[half],
        (((0,), (0,)), ((), ())),
        precision=HIGHEST,
        preferred_element_type=F32,
    )
    q = lax.broadcasted_iota(jnp.int32, (32, 64), 0) & 7 ^ FLIP_Q
    lane = lax.broadcasted_iota(jnp.int32, (32, 64), 1)
    own = base + half * 8
    across = base + 8 - half * 8
    boxes = [own + q, own + (q & ~2), own + (q | 2), own + (q & ~4), own + (q | 4), across + q]
    total = jnp.zeros((32, 128), F32)
    for v, box in enumerate(boxes):
        hot = jnp.where(lane == box, 1.0, 0.0).astype(F32)
        mine = jnp.dot(hot, picked, precision=HIGHEST, preferred_element_type=F32)
        total = total + mine * mask_ref[v : v + 1, :]
    for piece, part in pieces(total):
        out_ref[10, 32 * piece : 32 * piece + 32, :128] = part
    out_ref[11, :, :512] = pick_ref[...]


def prepare(nodes, cen):
    return pl.pallas_call(
        prepare_kernel,
        out_shape=jax.ShapeDtypeStruct((12, 96, K), BF16),
        in_specs=[VMEM] * 5,
        out_specs=VMEM,
        scratch_shapes=[pltpu.VMEM((10, 32, K), F32)],
        compiler_params=pltpu.CompilerParams(vmem_limit_bytes=6 * 2**20),
        cost_estimate=pl.CostEstimate(flops=10**7, bytes_accessed=5 * 2**20, transcendentals=0),
        name="prepare",
    )(nodes, cen, jnp.asarray(CENTRE), jnp.asarray(MASK), jnp.asarray(PICK, BF16))


def pack_kernel(coeffs_hbm, freqs_hbm, out_ref, coeffs_ref, freqs_ref, sems):
    freqs_copy = pltpu.make_async_copy(freqs_hbm, freqs_ref, sems.at[0])
    coeffs_copy = pltpu.make_async_copy(coeffs_hbm, coeffs_ref, sems.at[1])
    freqs_copy.start()
    coeffs_copy.start()

    def spread(rows):
        i = lax.broadcasted_iota(jnp.int32, (rows, rows), 0)
        j = lax.broadcasted_iota(jnp.int32, (rows, rows), 1)
        half = rows // 2
        return jnp.where(i == 2 * (j % half) + j // half, 1.0, 0.0).astype(BF16)

    def turned(x, y):
        z = lax.dot_general(x, y, (((0,), (0,)), ((), ())), preferred_element_type=F32)
        z = z.reshape(32, 4, z.shape[1])
        if FLIP_CHUNK:
            z = jnp.concatenate([z[i ^ FLIP_CHUNK : (i ^ FLIP_CHUNK) + 1] for i in range(32)], axis=0)
        return z.astype(BF16)

    whole, tail = spread(256), spread(128)
    freqs_copy.wait()
    i = lax.broadcasted_iota(jnp.int32, (10, 128), 0)
    j = lax.broadcasted_iota(jnp.int32, (10, 128), 1)
    position = lax.axis_index(NEAR) ^ FLIP_NEAR
    spot = SPOTS + 4 * (position & 15)
    hot = (i == j) | ((i > 5) & (j == i - 6 + spot))
    freqs = freqs_ref[...].astype(F32).reshape(10, COLS).astype(BF16)
    out_ref[:, :, 1152:] = turned(freqs, jnp.where(hot, 1.0, 0.0).astype(BF16))
    coeffs_copy.wait()
    for m in range(4):
        z = turned(coeffs_ref[m * 256 : m * 256 + 256, :], whole)
        out_ref[:, :, m * 128 : m * 128 + 128] = z[:, :, :128]
        out_ref[:, :, 512 + m * 128 : 512 + m * 128 + 128] = z[:, :, 128:]
    out_ref[:, :, 1024:1152] = turned(coeffs_ref[1024:1152, :], tail)


def pack(coeffs, freqs):
    return pl.pallas_call(
        pack_kernel,
        out_shape=jax.ShapeDtypeStruct((32, 4, WIDE), BF16),
        in_specs=[pl.BlockSpec(memory_space=pl.ANY)] * 2,
        out_specs=VMEM,
        scratch_shapes=[
            pltpu.VMEM((2 * K, COLS), BF16),
            pltpu.VMEM((5, 2, COLS), BF16),
            pltpu.SemaphoreType.DMA((2,)),
        ],
        compiler_params=pltpu.CompilerParams(vmem_limit_bytes=PACK_VMEM),
        cost_estimate=pl.CostEstimate(flops=10**7, bytes_accessed=2**20, transcendentals=0),
        name="pack",
    )(coeffs, freqs)


def horner(coefficients, u):
    total = u * coefficients[-1] + coefficients[-2]
    for value in coefficients[-3::-1]:
        total = total * u + value
    return total


def cos_sin(turns):
    r = turns - jnp.floor(turns + 0.5)
    u = r * r
    sine = r * horner(SIN, u)
    return 1.0 - sine * sine, sine * horner(COS, u)


def dot(a, b):
    return lax.dot_general(a, b, (((1,), (1,)), ((), ())), preferred_element_type=F32)


def block(q):
    return slice(q * 16, q * 16 + 16)


def pieces(rest):
    for _ in range(3):
        part = rest.astype(BF16)
        yield part
        rest = rest - part.astype(F32)


def picked(table_ref, rows, freq):
    pick = table_ref[11, 16 * rows : 16 * rows + 16, :256]
    return jnp.dot(freq, pick, preferred_element_type=F32)


def phases(placed, table_ref, sets, t_ref):
    lanes = placed[:, :96].astype(BF16)
    i = lax.broadcasted_iota(jnp.int32, (128, 128), 0)
    j = lax.broadcasted_iota(jnp.int32, (128, 128), 1)
    first = jnp.where(i < 4, i // 2, (i - 4) // 4 + 2)
    gather = jnp.where((first == j) & (i < len(TERMS)), 1.0, 0.0).astype(F32)
    high, mid, low = (table_ref[10, 32 * p : 32 * p + 32, :128].astype(F32) for p in range(3))
    centre = high + mid + low
    centre = jnp.concatenate(
        [jnp.broadcast_to(centre[q : q + 1], (16, 128)) for q in range(8)], axis=0
    )
    const = sum(
        jnp.dot(part, gather.astype(BF16), preferred_element_type=F32)
        for part in pieces(placed[:, 128:] * centre)
    )
    for i, s in enumerate(sets):
        t_ref[i] = jnp.dot(lanes, table_ref[s], preferred_element_type=F32) + const[:, s : s + 1]


def rotated(turns, re, im):
    c, s = cos_sin(turns)
    return c * re - s * im, s * re + c * im


def contribution(state_ref, turns_ref, first, mine, w_ref, s_ref):
    for q in range(8):
        here = block(q)
        re, im = rotated(turns_ref[first, here, :], state_ref[here, :], state_ref[block(q + 8), :])
        w_ref[here, :] = re.astype(BF16)
        w_ref[block(q + 8), :] = im.astype(BF16)
    s_ref[...] = dot(w_ref[...], mine)
    for q in range(8):
        here = block(q)
        c, s = cos_sin(turns_ref[first + 1, here, :])
        v = c * s_ref[here, :] - s * s_ref[block(q + 8), :]
        w_ref[here, :] = v.astype(BF16)
    a = lax.broadcasted_iota(jnp.int32, (32, COLS), 0)
    b = lax.broadcasted_iota(jnp.int32, (32, COLS), 1)
    box = b // 16 ^ FLIP_Q ^ FLIP_BACK
    angles = jnp.where((a // 4 == box) & (a % 4 == b % 4), 1.0, 0.0).astype(BF16)
    return jnp.dot(angles, w_ref[:COLS, :], preferred_element_type=F32).astype(BF16)


def fields(field_ref, q):
    x = field_ref[4 * q : 4 * q + 4].astype(F32).reshape(16, WIDE)
    re = jnp.concatenate([x[:, :512], x[:, 1024:1088]], axis=1)
    im = jnp.concatenate([x[:, 512:1024], x[:, 1088:1152]], axis=1)
    return re, im


def lanes_16(freq_ref):
    return freq_ref[...].astype(F32).reshape(COLS, 128)[:, :16].astype(BF16)


def own_kernel(
    field_ref, freq_ref, table_ref, interp_ref, v_ref, s_ref, low_ref, high_ref, last_ref, t_ref
):
    freq = lanes_16(freq_ref)
    sources = [
        jnp.concatenate([freq[block(moved(q, rows))] for q in range(8)], axis=0)
        for rows in range(ACROSS)
    ]
    placed = jnp.dot(
        jnp.concatenate(sources, axis=1),
        table_ref[11, : 16 * ACROSS, :256],
        preferred_element_type=F32,
    )
    phases(placed, table_ref, range(HERE), t_ref)

    for level in range(3):
        for q in range(8):
            here = block(q)
            for kind, w_ref in enumerate((low_ref, high_ref)):
                src = child(q, level, kind)
                if level == 0:
                    re, im = fields(field_ref, src)
                else:
                    re = s_ref[block(src), :]
                    im = s_ref[block(src + 8), :]
                re, im = rotated(t_ref[2 * level + kind, here, :], re, im)
                w_ref[here, :] = re.astype(BF16)
                w_ref[block(q + 8), :] = im.astype(BF16)
        s_ref[...] = dot(low_ref[...], interp_ref[0]) + dot(high_ref[...], interp_ref[1])
    mine = interp_ref[lax.axis_index("z4")]
    v_ref[...] = contribution(s_ref, t_ref, 6, mine, low_ref, last_ref)


def across_kernel(
    freq_ref,
    freq_across_ref,
    v_ref,
    s_ref,
    table_ref,
    interp_ref,
    eval_ref,
    out_ref,
    w_ref,
    last_ref,
    t_ref,
):
    half = lax.axis_index("z4")
    place = half ^ (FLIP_ALL >> 6)
    placed = picked(table_ref, OWN, lanes_16(freq_ref))
    across = freq_across_ref[...].astype(F32)[:, None]
    across = jnp.broadcast_to(across, (2, 16, 4, 128)).reshape(COLS, 128)
    across = across[:, SPOTS : SPOTS + 64]
    a = lax.broadcasted_iota(jnp.int32, (COLS, 64), 0)
    b = lax.broadcasted_iota(jnp.int32, (COLS, 64), 1)
    across = jnp.where(a // 4 % 16 == b // 4, across, 0.0).astype(BF16)
    placed = placed + jnp.dot(across, table_ref[11, :64, 256:512], preferred_element_type=F32)
    phases(placed, table_ref, (HERE, HERE + 1), t_ref)
    v = contribution(s_ref, t_ref, 0, interp_ref[half], w_ref, last_ref)
    both = jnp.concatenate([v_ref[...], v], axis=0)
    both = jnp.dot(both, eval_ref[...], preferred_element_type=F32)
    for where, part in ((place, both[:32]), (1 - place, both[32:])):
        part = part.reshape(8, 4, PIX).astype(BF16)
        for p in range(8):
            member = p ^ FLIP_ALL & 7
            out_ref[where, :, p] = part[:, :, member * 128 : member * 128 + 128]


def own_levels(field, freq, table, interp):
    return pl.pallas_call(
        own_kernel,
        out_shape=[
            jax.ShapeDtypeStruct((32, K), BF16),
            jax.ShapeDtypeStruct((2 * COLS, K), F32),
        ],
        in_specs=[VMEM] * 4,
        out_specs=[VMEM] * 2,
        scratch_shapes=[
            pltpu.VMEM((2 * COLS, K), BF16),
            pltpu.VMEM((2 * COLS, K), BF16),
            pltpu.VMEM((2 * COLS, K), F32),
            pltpu.VMEM((HERE, COLS, K), F32),
        ],
        compiler_params=pltpu.CompilerParams(vmem_limit_bytes=8 * 2**20),
        cost_estimate=pl.CostEstimate(
            flops=8 * 2 * K * K * 256, bytes_accessed=10 * 2**20, transcendentals=0
        ),
        name="own_levels",
    )(field, freq, table, interp)


def across_level(freq, freq_across, v, state, table, interp, evaluate):
    return pl.pallas_call(
        across_kernel,
        out_shape=jax.ShapeDtypeStruct((2, 8, 8, 4, 128), BF16),
        in_specs=[VMEM] * 7,
        out_specs=VMEM,
        scratch_shapes=[
            pltpu.VMEM((2 * COLS, K), BF16),
            pltpu.VMEM((2 * COLS, K), F32),
            pltpu.VMEM((2, COLS, K), F32),
        ],
        compiler_params=pltpu.CompilerParams(vmem_limit_bytes=6 * 2**20),
        cost_estimate=pl.CostEstimate(
            flops=2 * 2 * K * K * 256, bytes_accessed=5 * 2**20, transcendentals=0
        ),
        name="across_level",
    )(freq, freq_across, v, state, table, interp, evaluate)


def exchange(block, axes, flip):
    groups = [[i ^ flip for i in range(block.shape[0])]]
    return lax.all_to_all(
        block, axes, split_axis=0, concat_axis=0, tiled=True, axis_index_groups=groups
    )


def body(coeffs, freqs, nodes, centres, interp, evaluate):
    field = exchange(pack(coeffs.reshape(2 * K, COLS), freqs[0]), NEAR, FLIP_NEAR)
    freq = field[:, :, WIDE - 128 :]
    spots = jnp.sum(freq.reshape(2, 16, 4, 128).astype(F32), axis=1).astype(BF16)
    freq_across = lax.ppermute(spots, "z4", [(0, 1), (1, 0)])
    table = prepare(nodes.reshape(24, K), centres.reshape(24, 64))
    v, state = own_levels(field, freq, table, interp)
    part = across_level(freq, freq_across, v, state, table, interp, evaluate.T)
    part = part.reshape(128, 4, 128)
    part = exchange(part, ALL, FLIP_ALL)
    total = jnp.sum(part.reshape(2, 8, 2, 4, 4, 128).astype(F32), axis=(0, 2))
    return total.reshape(COLS, 128).T


def solution(mesh):
    fine = Mesh(mesh.devices.reshape(SIZES), AXES)
    box, ang = ("y", "z4", "z2", "z1", "c"), ("zh", "x")
    return jax.shard_map(
        body,
        mesh=fine,
        in_specs=(P(ang, None, None, box), P(ang, None, None, box), P(), P(), P(), P()),
        out_specs=P(ang, box),
        check_vma=False,
    )
```

```python
import jax
import jax.numpy as jnp
import numpy as np
from jax import lax
from jax.experimental import pallas as pl
from jax.experimental.pallas import tpu as pltpu
from jax.sharding import Mesh, PartitionSpec as P

AXES = ("y", "z4", "z2", "z1", "c", "zh", "x")
SIZES = (4, 2, 2, 2, 2, 2, 4)
NEAR = ("z2", "z1", "c", "x")
ALL = ("z4", "z2", "z1", "c", "zh", "x")
FLIP_NEAR = 10
FLIP_ALL = 6
FLIP_Q = FLIP_NEAR >> 2
FLIP_BACK = FLIP_ALL >> 3 & 7
FLIP_CHUNK = FLIP_NEAR ^ (FLIP_BACK << 2 | FLIP_ALL & 3)
SPOTS = 16
K = 576
WIDE = 1280
PACK_VMEM = 60 * 2**20
COLS = 128
PIX = 1024
F32 = jnp.float32
BF16 = jnp.bfloat16
HIGHEST = lax.Precision.HIGHEST
VMEM = pl.BlockSpec(memory_space=pltpu.VMEM)

COS = (
    1.4142134962552286,
    -6.978850948563802,
    5.739460376906949,
    -1.8835579059851506,
    0.31068802752335445,
)
SIN = (
    4.442882919124345,
    -7.308245686509067,
    3.6063542184329913,
    -0.8461116503747359,
    0.10982451642751799,
)

OWN, LOW1, HIGH1, LOW2, HIGH2, ACROSS = range(6)
FREQS = []


def lanes_of(rows, level):
    FREQS.extend((rows, level, d) for d in range(2))
    return len(FREQS) - 2


F0, F1, F2, F3, F4 = (lanes_of(OWN, level) for level in range(5))
UP1 = lanes_of(LOW1, 0), lanes_of(HIGH1, 0)
UP2 = lanes_of(LOW2, 1), lanes_of(HIGH2, 1)
A3, A4 = (lanes_of(ACROSS, level) for level in (3, 4))

SETS = [
    [(-1, F0, 0, 0)],
    [(-1, F0, 0, 1)],
    [(1, UP1[0], 0, 2), (-1, F1, 1, 0)],
    [(1, UP1[1], 0, 2), (-1, F1, 1, 1)],
    [(1, UP2[0], 1, 2), (-1, F2, 2, 0)],
    [(1, UP2[1], 1, 2), (-1, F2, 2, 1)],
    [(1, F2, 2, 2), (-1, F3, 3, None)],
    [(1, F3, 3, 2), (1, F4, 3, 2)],
    [(1, F2, 2, 2), (-1, A3, 3, None)],
    [(1, A3, 3, 2), (1, A4, 3, 2)],
]
HERE = 8
TERMS = [
    (s, sign, lane + d, level, kind, d)
    for s, terms in enumerate(SETS)
    for sign, lane, level, kind in terms
    for d in range(2)
]


def tables():
    pick = np.zeros((6, 16, 256), np.float32)
    for lane, (rows, level, d) in enumerate(FREQS):
        at = level * 2 + d
        for piece in range(3):
            pick[rows, at, 32 * piece + lane] = 1
        for i, term in enumerate(TERMS):
            if term[2] == lane:
                pick[rows, at, 128 + i] = 1
    spots = np.zeros((96, 256), np.float32)
    for i in range(64):
        spots[i] = pick[ACROSS, 6 + i % 4]
    centre = np.zeros((2, 24, 128), np.float32)
    mask = np.zeros((8, 128), np.float32)
    for i, (s, sign, lane, level, kind, d) in enumerate(TERMS):
        for half in range(2):
            k = half if kind is None else kind
            centre[half, (level * 3 + k) * 2 + d, i] = sign
        mask[FREQS[lane][0], i] = 1
    pick = np.concatenate([pick.reshape(96, 256), spots], axis=1)
    return pick, centre, mask


PICK, CENTRE, MASK = tables()


def moved(q, rows):
    box = q ^ FLIP_Q
    box = {OWN: box, LOW1: box & ~2, HIGH1: box | 2, LOW2: box & ~4, HIGH2: box | 4}[rows]
    return box ^ FLIP_Q


def child(q, level, kind):
    box = q ^ FLIP_Q
    return ((box & ~(1 << level)) | (kind << level)) ^ FLIP_Q


def prepare_kernel(nodes_ref, cen_ref, centre_ref, mask_ref, pick_ref, out_ref, wide_ref):
    base = lax.axis_index("y") * 16
    half = lax.axis_index("z4")
    turn = 0.5 / np.pi

    def pieces(rest):
        for piece in range(3):
            part = rest.astype(BF16)
            yield piece, part
            rest = rest - part.astype(F32)

    wide_ref[...] = jnp.zeros_like(wide_ref)
    for s, sign, lane, level, kind, d in TERMS:

        def row(kind):
            i = (level * 3 + kind) * 2 + d
            return nodes_ref[i : i + 1, :]

        value = jnp.where(half == 0, row(0), row(1)) if kind is None else row(kind)
        wide_ref[s, lane : lane + 1, :] = value * (sign * turn)
    for s in range(len(SETS)):
        for piece, part in pieces(wide_ref[s]):
            out_ref[s, 32 * piece : 32 * piece + 32, :] = part

    picked = lax.dot_general(
        cen_ref[...] * turn,
        centre_ref[half],
        (((0,), (0,)), ((), ())),
        precision=HIGHEST,
        preferred_element_type=F32,
    )
    q = lax.broadcasted_iota(jnp.int32, (32, 64), 0) & 7 ^ FLIP_Q
    lane = lax.broadcasted_iota(jnp.int32, (32, 64), 1)
    own = base + half * 8
    across = base + 8 - half * 8
    boxes = [own + q, own + (q & ~2), own + (q | 2), own + (q & ~4), own + (q | 4), across + q]
    total = jnp.zeros((32, 128), F32)
    for v, box in enumerate(boxes):
        hot = jnp.where(lane == box, 1.0, 0.0).astype(F32)
        mine = jnp.dot(hot, picked, precision=HIGHEST, preferred_element_type=F32)
        total = total + mine * mask_ref[v : v + 1, :]
    for piece, part in pieces(total):
        out_ref[10, 32 * piece : 32 * piece + 32, :128] = part
    out_ref[11, :, :512] = pick_ref[...]


def prepare(nodes, cen):
    return pl.pallas_call(
        prepare_kernel,
        out_shape=jax.ShapeDtypeStruct((12, 96, K), BF16),
        in_specs=[VMEM] * 5,
        out_specs=VMEM,
        scratch_shapes=[pltpu.VMEM((10, 32, K), F32)],
        compiler_params=pltpu.CompilerParams(vmem_limit_bytes=6 * 2**20),
        cost_estimate=pl.CostEstimate(flops=10**7, bytes_accessed=5 * 2**20, transcendentals=0),
        name="prepare",
    )(nodes, cen, jnp.asarray(CENTRE), jnp.asarray(MASK), jnp.asarray(PICK, BF16))


def pack_kernel(coeffs_hbm, freqs_hbm, out_ref, coeffs_ref, freqs_ref, sems):
    freqs_copy = pltpu.make_async_copy(freqs_hbm, freqs_ref, sems.at[0])
    coeffs_copy = pltpu.make_async_copy(coeffs_hbm, coeffs_ref, sems.at[1])
    freqs_copy.start()
    coeffs_copy.start()

    def spread(rows):
        i = lax.broadcasted_iota(jnp.int32, (rows, rows), 0)
        j = lax.broadcasted_iota(jnp.int32, (rows, rows), 1)
        half = rows // 2
        return jnp.where(i == 2 * (j % half) + j // half, 1.0, 0.0).astype(BF16)

    def turned(x, y):
        z = lax.dot_general(x, y, (((0,), (0,)), ((), ())), preferred_element_type=F32)
        z = z.reshape(32, 4, z.shape[1])
        if FLIP_CHUNK:
            z = jnp.concatenate([z[i ^ FLIP_CHUNK : (i ^ FLIP_CHUNK) + 1] for i in range(32)], axis=0)
        return z.astype(BF16)

    whole, tail = spread(256), spread(128)
    freqs_copy.wait()
    i = lax.broadcasted_iota(jnp.int32, (10, 128), 0)
    j = lax.broadcasted_iota(jnp.int32, (10, 128), 1)
    position = lax.axis_index(NEAR) ^ FLIP_NEAR
    spot = SPOTS + 4 * (position & 15)
    hot = (i == j) | ((i > 5) & (j == i - 6 + spot))
    freqs = freqs_ref[...].astype(F32).reshape(10, COLS).astype(BF16)
    out_ref[:, :, 1152:] = turned(freqs, jnp.where(hot, 1.0, 0.0).astype(BF16))
    coeffs_copy.wait()
    for m in range(4):
        z = turned(coeffs_ref[m * 256 : m * 256 + 256, :], whole)
        out_ref[:, :, m * 128 : m * 128 + 128] = z[:, :, :128]
        out_ref[:, :, 512 + m * 128 : 512 + m * 128 + 128] = z[:, :, 128:]
    out_ref[:, :, 1024:1152] = turned(coeffs_ref[1024:1152, :], tail)


def pack(coeffs, freqs):
    return pl.pallas_call(
        pack_kernel,
        out_shape=jax.ShapeDtypeStruct((32, 4, WIDE), BF16),
        in_specs=[pl.BlockSpec(memory_space=pl.ANY)] * 2,
        out_specs=VMEM,
        scratch_shapes=[
            pltpu.VMEM((2 * K, COLS), BF16),
            pltpu.VMEM((5, 2, COLS), BF16),
            pltpu.SemaphoreType.DMA((2,)),
        ],
        compiler_params=pltpu.CompilerParams(vmem_limit_bytes=PACK_VMEM),
        cost_estimate=pl.CostEstimate(flops=10**7, bytes_accessed=2**20, transcendentals=0),
        name="pack",
    )(coeffs, freqs)


def horner(coefficients, u):
    total = u * coefficients[-1] + coefficients[-2]
    for value in coefficients[-3::-1]:
        total = total * u + value
    return total


def cos_sin(turns):
    r = turns - jnp.floor(turns + 0.5)
    u = r * r
    sine = r * horner(SIN, u)
    return 1.0 - sine * sine, sine * horner(COS, u)


def dot(a, b):
    return lax.dot_general(a, b, (((1,), (1,)), ((), ())), preferred_element_type=F32)


def block(q):
    return slice(q * 16, q * 16 + 16)


def pieces(rest):
    for _ in range(3):
        part = rest.astype(BF16)
        yield part
        rest = rest - part.astype(F32)


def picked(table_ref, rows, freq):
    pick = table_ref[11, 16 * rows : 16 * rows + 16, :256]
    return jnp.dot(freq, pick, preferred_element_type=F32)


def phases(placed, table_ref, sets, t_ref):
    lanes = placed[:, :96].astype(BF16)
    i = lax.broadcasted_iota(jnp.int32, (128, 128), 0)
    j = lax.broadcasted_iota(jnp.int32, (128, 128), 1)
    first = jnp.where(i < 4, i // 2, (i - 4) // 4 + 2)
    gather = jnp.where((first == j) & (i < len(TERMS)), 1.0, 0.0).astype(F32)
    high, mid, low = (table_ref[10, 32 * p : 32 * p + 32, :128].astype(F32) for p in range(3))
    centre = high + mid + low
    centre = jnp.concatenate(
        [jnp.broadcast_to(centre[q : q + 1], (16, 128)) for q in range(8)], axis=0
    )
    const = sum(
        jnp.dot(part, gather.astype(BF16), preferred_element_type=F32)
        for part in pieces(placed[:, 128:] * centre)
    )
    for i, s in enumerate(sets):
        t_ref[i] = jnp.dot(lanes, table_ref[s], preferred_element_type=F32) + const[:, s : s + 1]


def rotated(turns, re, im):
    c, s = cos_sin(turns)
    return c * re - s * im, s * re + c * im


def contribution(state_ref, turns_ref, first, mine, w_ref, s_ref):
    for q in range(8):
        here = block(q)
        re, im = rotated(turns_ref[first, here, :], state_ref[here, :], state_ref[block(q + 8), :])
        w_ref[here, :] = re.astype(BF16)
        w_ref[block(q + 8), :] = im.astype(BF16)
    s_ref[...] = dot(w_ref[...], mine)
    for q in range(8):
        here = block(q)
        c, s = cos_sin(turns_ref[first + 1, here, :])
        v = c * s_ref[here, :] - s * s_ref[block(q + 8), :]
        w_ref[here, :] = v.astype(BF16)
    a = lax.broadcasted_iota(jnp.int32, (32, COLS), 0)
    b = lax.broadcasted_iota(jnp.int32, (32, COLS), 1)
    box = b // 16 ^ FLIP_Q ^ FLIP_BACK
    angles = jnp.where((a // 4 == box) & (a % 4 == b % 4), 1.0, 0.0).astype(BF16)
    return jnp.dot(angles, w_ref[:COLS, :], preferred_element_type=F32).astype(BF16)


def fields(field_ref, q):
    x = field_ref[4 * q : 4 * q + 4].astype(F32).reshape(16, WIDE)
    re = jnp.concatenate([x[:, :512], x[:, 1024:1088]], axis=1)
    im = jnp.concatenate([x[:, 512:1024], x[:, 1088:1152]], axis=1)
    return re, im


def lanes_16(freq_ref):
    return freq_ref[...].astype(F32).reshape(COLS, 128)[:, :16].astype(BF16)


def own_kernel(
    field_ref, freq_ref, table_ref, interp_ref, v_ref, s_ref, low_ref, high_ref, last_ref, t_ref
):
    freq = lanes_16(freq_ref)
    sources = [
        jnp.concatenate([freq[block(moved(q, rows))] for q in range(8)], axis=0)
        for rows in range(ACROSS)
    ]
    placed = jnp.dot(
        jnp.concatenate(sources, axis=1),
        table_ref[11, : 16 * ACROSS, :256],
        preferred_element_type=F32,
    )
    phases(placed, table_ref, range(HERE), t_ref)

    for level in range(3):
        for q in range(8):
            here = block(q)
            for kind, w_ref in enumerate((low_ref, high_ref)):
                src = child(q, level, kind)
                if level == 0:
                    re, im = fields(field_ref, src)
                else:
                    re = s_ref[block(src), :]
                    im = s_ref[block(src + 8), :]
                re, im = rotated(t_ref[2 * level + kind, here, :], re, im)
                w_ref[here, :] = re.astype(BF16)
                w_ref[block(q + 8), :] = im.astype(BF16)
        s_ref[...] = dot(low_ref[...], interp_ref[0]) + dot(high_ref[...], interp_ref[1])
    mine = interp_ref[lax.axis_index("z4")]
    v_ref[...] = contribution(s_ref, t_ref, 6, mine, low_ref, last_ref)


def across_kernel(
    freq_ref,
    freq_across_ref,
    v_ref,
    s_ref,
    table_ref,
    interp_ref,
    eval_ref,
    out_ref,
    w_ref,
    last_ref,
    t_ref,
):
    half = lax.axis_index("z4")
    place = half ^ (FLIP_ALL >> 6)
    placed = picked(table_ref, OWN, lanes_16(freq_ref))
    across = freq_across_ref[...].astype(F32)[:, None]
    across = jnp.broadcast_to(across, (2, 16, 4, 128)).reshape(COLS, 128)
    across = across[:, SPOTS : SPOTS + 64]
    a = lax.broadcasted_iota(jnp.int32, (COLS, 64), 0)
    b = lax.broadcasted_iota(jnp.int32, (COLS, 64), 1)
    across = jnp.where(a // 4 % 16 == b // 4, across, 0.0).astype(BF16)
    placed = placed + jnp.dot(across, table_ref[11, :64, 256:512], preferred_element_type=F32)
    phases(placed, table_ref, (HERE, HERE + 1), t_ref)
    v = contribution(s_ref, t_ref, 0, interp_ref[half], w_ref, last_ref)
    both = jnp.concatenate([v_ref[...], v], axis=0)
    both = jnp.dot(both, eval_ref[...], preferred_element_type=F32)
    for where, part in ((place, both[:32]), (1 - place, both[32:])):
        part = part.reshape(8, 4, PIX).astype(BF16)
        for p in range(8):
            member = p ^ FLIP_ALL & 7
            out_ref[where, :, p] = part[:, :, member * 128 : member * 128 + 128]


def own_levels(field, freq, table, interp):
    return pl.pallas_call(
        own_kernel,
        out_shape=[
            jax.ShapeDtypeStruct((32, K), BF16),
            jax.ShapeDtypeStruct((2 * COLS, K), F32),
        ],
        in_specs=[VMEM] * 4,
        out_specs=[VMEM] * 2,
        scratch_shapes=[
            pltpu.VMEM((2 * COLS, K), BF16),
            pltpu.VMEM((2 * COLS, K), BF16),
            pltpu.VMEM((2 * COLS, K), F32),
            pltpu.VMEM((HERE, COLS, K), F32),
        ],
        compiler_params=pltpu.CompilerParams(vmem_limit_bytes=8 * 2**20),
        cost_estimate=pl.CostEstimate(
            flops=8 * 2 * K * K * 256, bytes_accessed=10 * 2**20, transcendentals=0
        ),
        name="own_levels",
    )(field, freq, table, interp)


def across_level(freq, freq_across, v, state, table, interp, evaluate):
    return pl.pallas_call(
        across_kernel,
        out_shape=jax.ShapeDtypeStruct((2, 8, 8, 4, 128), BF16),
        in_specs=[VMEM] * 7,
        out_specs=VMEM,
        scratch_shapes=[
            pltpu.VMEM((2 * COLS, K), BF16),
            pltpu.VMEM((2 * COLS, K), F32),
            pltpu.VMEM((2, COLS, K), F32),
        ],
        compiler_params=pltpu.CompilerParams(vmem_limit_bytes=6 * 2**20),
        cost_estimate=pl.CostEstimate(
            flops=2 * 2 * K * K * 256, bytes_accessed=5 * 2**20, transcendentals=0
        ),
        name="across_level",
    )(freq, freq_across, v, state, table, interp, evaluate)


def exchange(block, axes, flip):
    groups = [[i ^ flip for i in range(block.shape[0])]]
    return lax.all_to_all(
        block, axes, split_axis=0, concat_axis=0, tiled=True, axis_index_groups=groups
    )


def finish_kernel(part_ref, out_ref):
    total = jnp.zeros((8, 4, 4, 128), F32)
    for z4 in range(2):
        for zh in range(2):
            total = total + part_ref[z4, :, zh].astype(F32)
    out_ref[...] = total.reshape(COLS, 128).T


def finish(part):
    return pl.pallas_call(
        finish_kernel,
        out_shape=jax.ShapeDtypeStruct((128, COLS), F32),
        in_specs=[VMEM],
        out_specs=VMEM,
        compiler_params=pltpu.CompilerParams(vmem_limit_bytes=4 * 2**20),
        cost_estimate=pl.CostEstimate(flops=10**5, bytes_accessed=2**18, transcendentals=0),
        name="finish",
    )(part)


def body(coeffs, freqs, nodes, centres, interp, evaluate):
    field = exchange(pack(coeffs.reshape(2 * K, COLS), freqs[0]), NEAR, FLIP_NEAR)
    freq = field[:, :, WIDE - 128 :]
    spots = jnp.sum(freq.reshape(2, 16, 4, 128).astype(F32), axis=1).astype(BF16)
    freq_across = lax.ppermute(spots, "z4", [(0, 1), (1, 0)])
    table = prepare(nodes.reshape(24, K), centres.reshape(24, 64))
    v, state = own_levels(field, freq, table, interp)
    part = across_level(freq, freq_across, v, state, table, interp, evaluate.T)
    part = part.reshape(128, 4, 128)
    part = exchange(part, ALL, FLIP_ALL)
    return finish(part.reshape(2, 8, 2, 4, 4, 128))


def solution(mesh):
    fine = Mesh(mesh.devices.reshape(SIZES), AXES)
    box, ang = ("y", "z4", "z2", "z1", "c"), ("zh", "x")
    return jax.shard_map(
        body,
        mesh=fine,
        in_specs=(P(ang, None, None, box), P(ang, None, None, box), P(), P(), P(), P()),
        out_specs=P(ang, box),
        check_vma=False,
    )
```
